128 devices in a mesh: ctx: 16 (over z_lo, y, core), tp: 8 (over x, z_hi).
Axes of the slice: x: 4, y: 4, z: 4 (z_hi: 2, z_lo: 2; z = z_hi * 2 + z_lo), core: 2. Of those that a mesh axis runs over, the one named last changes fastest.
Arguments:
- tokens: bfloat16 [16384, 4096], P('ctx', 'tp'), may hold values from -6 to 6
- grad_out: bfloat16 [16384, 4096], P('ctx', 'tp'), may hold values from -1.1953125 to 1.1953125
- expert_ids: int32 [16384, 2], P(('ctx', 'tp')), may hold values from 0 to 63, all different within a row; in each aligned block of 128 rows (0 to 127, 128 to 255, ...) at most 6 rows name the same one
- gates: float32 [16384, 2], P(('ctx', 'tp')), may hold values from 0.1 to 1
- w_gate: bfloat16 [128, 4096, 768], P(('ctx', 'tp')), may hold values from -0.09375 to 0.09375
- w_up: bfloat16 [128, 4096, 768], P(('ctx', 'tp')), may hold values from -0.09375 to 0.09375
- w_down: bfloat16 [128, 768, 4096], P(('ctx', 'tp')), may hold values from -0.15625 to 0.15625
Outputs:
- grad_tokens: bfloat16 [16384, 4096], P('ctx', 'tp')
- grad_gates: float32 [16384, 2], P(('ctx', 'tp'))
The draws below stay inside these ranges and needn't reach their ends.
Inputs may be any that keep to these rules, and one draw needn't show every extreme that they name: `expert_ids`: in the 128 rows of one device no expert is named by more than 6 rows, a bound that some block reaches; the 2 experts of a row differ; every expert is named somewhere.
All inputs are finite; a program needn't handle non-finite values.
Results may differ from the reference program's by a relative error of at most 0.015.
Values may be sent and summed in bfloat16 or wider, within the bound.
A program may use at most 192 MiB of HBM per device.

```python
import math
import jax
import jax.numpy as jnp
import numpy as np
from jax import lax

D = 4096
FF = 1536
TOPK = 2
TOK_DEV = 128
SLAB_FF = 768
EXPERTS = 64
CAP = 6
TOKENS = 16384
N_CTX = 16
N_TP = 8


def block_levels(stream_key, shape, shards, smallest, largest):
    loudness = 1.0
    for position, parts in shards:
        draws = jax.random.uniform(jax.random.fold_in(jax.random.fold_in(stream_key, 6), position), (parts,), jnp.float32, smallest / len(shards), largest / len(shards))
        loudness = loudness * jnp.repeat(jnp.exp(draws), shape[position] // parts).reshape((-1,) + (1,) * (len(shape) - 1 - position))
    return loudness


def routed_block(own_key, own, number, rows, number_of, top, most, lean):
    ranking = jax.random.permutation(own_key, number_of)
    packed, usual = portions_of(number_of, rows * top, most, lean, True), portions_of(number_of, rows * top, most, lean, False)
    places = jnp.arange(number_of)

    def named(tallies, rotation):
        used = int((tallies > 0).sum())
        fixed = max(1, used // 4)
        passed = fixed + (places - fixed + rotation * (used - fixed)) % max(1, number_of - fixed)
        return jnp.zeros((number_of,), jnp.int32).at[ranking[jnp.where(places < fixed, places, passed)]].set(jnp.asarray(tallies, jnp.int32))

    tallies = jnp.where(number % 4 == 0, named(packed, number // 4), named(usual, number - number // 4 - 1))
    mixed = jax.random.permutation(jax.random.fold_in(own, 3), number_of)
    source_of, receiver = mixed[0:number_of // 2 * 2:2], mixed[1:number_of // 2 * 2:2]
    room = jnp.minimum(tallies[source_of] - 1, most - tallies[receiver]) // 2
    room = jnp.where((source_of == ranking[0]) | (receiver == ranking[0]) | (tallies[receiver] == 0), 0, jnp.maximum(room, 0))
    passed = jax.random.randint(jax.random.fold_in(own, 4), (number_of // 2,), 0, 1 << 20) % (room + 1)
    tallies = tallies.at[source_of].add(-passed).at[receiver].add(passed)
    members = jnp.searchsorted(jnp.cumsum(tallies), jnp.arange(rows * top), side="right").astype(jnp.int32)
    listing = members.reshape(top, rows).T
    listing = listing[jax.random.permutation(jax.random.fold_in(own, 1), rows)]
    rotation = jax.random.randint(jax.random.fold_in(own, 2), (rows, 1), 0, top)
    return jnp.take_along_axis(listing, (jnp.arange(top)[None, :] + rotation) % top, axis=1)


def portions_of(count, total, most, skew, full):
    weights = [(1 << 20) // math.isqrt(grade ** skew) + 1 for grade in range(1, count + 1)]
    largest = most if full else min(most, max(-(-total // count), total * weights[0] // sum(weights)))
    least = 1 if total - largest >= count - 1 else 0
    given, rest = [largest] + [least] * (count - 1), total - largest - least * (count - 1)
    while rest > 0:
        movable = [i for i in range(1, count) if given[i] < largest] or [i for i in range(1, count) if given[i] < most]
        pool, budget = sum([weights[i] for i in movable]), rest
        for i in movable:
            extra = min(most - given[i], max(1, budget * weights[i] // pool), rest)
            given[i] = given[i] + extra
            rest = rest - extra
    return np.array(given)


def centred(key, shape, spread, most, shards=(), kind=jnp.bfloat16):
    gain = block_levels(key, shape, shards, -0.22, 0.18) if shards else 1.0
    entries = jax.random.normal(key, shape, jnp.float32) * spread * gain
    return jnp.minimum(jnp.maximum(entries, -most), most).astype(kind)


def setup_inputs(seed: int = 0) -> dict:
    seeds = jax.random.split(jax.random.key(seed), 8)
    tokens = centred(seeds[0], (TOKENS, D), 1.0, 6.0, ((0, 16), (1, 8)))
    grad_out = centred(seeds[1], (TOKENS, D), 0.2, 1.1953125, ((0, 16), (1, 8)))
    expert_ids_keys = jax.random.split(jax.random.fold_in(seeds[2], 1), TOKENS // TOK_DEV)
    expert_ids_turns = jax.random.permutation(jax.random.fold_in(seeds[2], 3), TOKENS // TOK_DEV)
    expert_ids = jax.vmap(lambda own, number: routed_block(jax.random.fold_in(seeds[2], 2), own, number, TOK_DEV, EXPERTS, TOPK, CAP, 2))(expert_ids_keys, expert_ids_turns).reshape((TOKENS, TOPK))
    gates = jnp.clip(jnp.exp(math.log(1.0) - 2.3025851 * jax.random.uniform(seeds[3], (TOKENS, TOPK), jnp.float32) ** block_levels(seeds[3], (TOKENS, TOPK), ((0, 128),), -0.2, 0.2)), 0.1, 1.0)
    w_gate = centred(seeds[4], (2 * EXPERTS, D, SLAB_FF), D ** -0.5, 0.09375, ((0, 128),))
    w_up = centred(seeds[5], (2 * EXPERTS, D, SLAB_FF), D ** -0.5, 0.09375, ((0, 128),))
    w_down = centred(seeds[6], (2 * EXPERTS, SLAB_FF, D), FF ** -0.5, 0.15625, ((0, 128),))
    return dict(tokens=tokens, grad_out=grad_out, expert_ids=expert_ids, gates=gates, w_gate=w_gate, w_up=w_up, w_down=w_down)


def reference(tokens, grad_out, expert_ids, gates, w_gate, w_up, w_down):
    flat = expert_ids.reshape(-1).astype(jnp.int32)
    order = jnp.argsort(flat, stable=True).astype(jnp.int32)
    counts = jnp.sum((flat[:, None] == jnp.arange(EXPERTS, dtype=jnp.int32)[None, :]).astype(jnp.int32), axis=0)
    starts = (jnp.cumsum(counts) - counts).astype(jnp.int32)
    limit = N_CTX * N_TP * CAP
    padded = jnp.concatenate([order, jnp.zeros((limit,), jnp.int32)])
    gate_flat = gates.reshape(-1)

    def one_expert(carry, expert):
        total_x, total_gate = carry
        index = lax.dynamic_slice(padded, (starts[expert],), (limit,))
        valid = jnp.arange(limit, dtype=jnp.int32) < counts[expert]
        token_row = index // TOPK
        rows_x = jnp.where(valid[:, None], tokens[token_row], jnp.zeros((), tokens.dtype))
        rows_dy = jnp.where(valid[:, None], grad_out[token_row], jnp.zeros((), grad_out.dtype))
        gate_sum = jnp.zeros((limit,), jnp.float32)
        halves = []
        for half in range(2):
            slab = 2 * expert + half
            gate_w = w_gate[slab]
            up_w = w_up[slab]
            down_w = w_down[slab]
            pre_a = jnp.dot(rows_x, gate_w, preferred_element_type=jnp.float32)
            pre_b = jnp.dot(rows_x, up_w, preferred_element_type=jnp.float32)
            sigma = jax.nn.sigmoid(pre_a)
            active = pre_a * sigma
            hidden = (active * pre_b).astype(jnp.bfloat16)
            produced = jnp.dot(hidden, down_w, preferred_element_type=jnp.float32)
            gate_sum = gate_sum + jnp.sum(produced * rows_dy.astype(jnp.float32), axis=1)
            back_h = jnp.dot(rows_dy, down_w.T, preferred_element_type=jnp.float32)
            d_a = (back_h * pre_b * sigma * (1.0 + pre_a * (1.0 - sigma))).astype(jnp.bfloat16)
            d_b = (back_h * active).astype(jnp.bfloat16)
            part_x = (jnp.dot(d_a, gate_w.T, preferred_element_type=jnp.float32)
                      + jnp.dot(d_b, up_w.T, preferred_element_type=jnp.float32)).astype(jnp.bfloat16)
            halves.append(part_x)
        pair_x = (halves[0].astype(jnp.float32) + halves[1].astype(jnp.float32)).astype(jnp.bfloat16)
        weight = jnp.where(valid, gate_flat[index], jnp.zeros((), jnp.float32))
        total_x = total_x.at[token_row].add(weight[:, None] * pair_x.astype(jnp.float32))
        total_gate = total_gate.at[index].add(jnp.where(valid, gate_sum, jnp.zeros((), jnp.float32)))
        return (total_x, total_gate), None

    start = (jnp.zeros(tokens.shape, jnp.float32), jnp.zeros(flat.shape, jnp.float32))
    (total_x, total_gate), unused = lax.scan(one_expert, start, jnp.arange(EXPERTS, dtype=jnp.int32))
    return total_x.astype(jnp.bfloat16), total_gate.reshape(TOKENS, TOPK)
```

```python
import jax
import jax.numpy as jnp
from jax import lax
from jax.sharding import PartitionSpec as P


def contract_last(left, right):
    return lax.dot_general(
        left, right, (((1,), (1,)), ((), ())), preferred_element_type=jnp.float32
    )


def body(tokens, grad_out, expert_ids, gates, w_gate, w_up, w_down):
    width_tp = lax.axis_size("tp")
    width_ctx = lax.axis_size("ctx")
    slabs = width_ctx * width_tp
    experts = slabs // 2
    tok_rows, topk = expert_ids.shape
    cap = 6
    group = cap * width_tp
    group_rows, shard = tokens.shape
    onehot = (expert_ids[:, :, None] == jnp.arange(experts, dtype=jnp.int32)).astype(jnp.float32)
    member = jnp.sum(onehot, axis=1)
    lower = (jnp.arange(tok_rows)[:, None] > jnp.arange(tok_rows)[None, :]).astype(jnp.float32)
    earlier = jnp.dot(lower, member)
    slot = jnp.sum(earlier[:, None, :] * onehot, axis=2).astype(jnp.int32)
    block = lax.axis_index("tp")
    position = expert_ids * group + block * cap + slot
    packed = jnp.concatenate([position.astype(jnp.float32), gates], axis=1)
    packed = lax.all_gather(packed, "tp", axis=0, tiled=True)
    pos = packed[:, :topk].astype(jnp.int32)
    gate_all = packed[:, topk:]
    places = jnp.arange(experts * group, dtype=jnp.int32)
    hit = places[:, None, None] == pos.T[None, :, :]
    select = jnp.any(hit, axis=1).astype(jnp.bfloat16)
    weigh = jnp.sum(jnp.where(hit, gate_all.T[None], 0.0), axis=1).astype(jnp.bfloat16)

    def dispatch(rows):
        picked = jnp.dot(select, rows, preferred_element_type=jnp.float32).astype(jnp.bfloat16)
        picked = jnp.broadcast_to(
            picked.reshape(experts, 1, group, shard), (experts, 2, group, shard)
        ).reshape(slabs, group, shard)
        got = lax.all_to_all(picked, ("ctx", "tp"), split_axis=0, concat_axis=0, tiled=True)
        got = got.reshape(width_ctx, width_tp, group, shard).transpose(0, 2, 1, 3)
        return got.reshape(width_ctx * group, width_tp * shard)

    rows_x = dispatch(tokens)
    rows_dy = dispatch(grad_out)
    gate_w = w_gate[0]
    up_w = w_up[0]
    down_w = w_down[0]
    pre_a = jnp.dot(rows_x, gate_w, preferred_element_type=jnp.float32)
    pre_b = jnp.dot(rows_x, up_w, preferred_element_type=jnp.float32)
    sigma = jax.nn.sigmoid(pre_a)
    active = pre_a * sigma
    back_h = contract_last(rows_dy, down_w)
    hidden = (active * pre_b).astype(jnp.bfloat16).astype(jnp.float32)
    part_gate = jnp.sum(hidden * back_h, axis=1)
    d_a = (back_h * pre_b * sigma * (1.0 + pre_a * (1.0 - sigma))).astype(jnp.bfloat16)
    d_b = (back_h * active).astype(jnp.bfloat16)
    part_x = (contract_last(d_a, gate_w) + contract_last(d_b, up_w)).astype(jnp.bfloat16)
    part_x = part_x.reshape(width_ctx, group, width_tp, shard).transpose(0, 2, 1, 3)
    part_x = part_x.reshape(slabs, group, shard)
    back_x = lax.all_to_all(part_x, ("ctx", "tp"), split_axis=0, concat_axis=0, tiled=True)
    back_gate = lax.all_to_all(
        part_gate.astype(jnp.bfloat16).reshape(slabs, cap), ("ctx", "tp"),
        split_axis=0, concat_axis=0, tiled=True,
    ).astype(jnp.float32)
    back_x = back_x.reshape(experts, 2, group, shard).astype(jnp.float32)
    pair_x = (back_x[:, 0] + back_x[:, 1]).astype(jnp.bfloat16).reshape(experts * group, shard)
    grad_tokens = lax.dot_general(
        weigh, pair_x, (((0,), (0,)), ((), ())), preferred_element_type=jnp.float32
    ).astype(jnp.bfloat16)
    back_gate = jnp.sum(back_gate.reshape(experts, 2, cap), axis=1).reshape(experts * cap)
    grad_gates = back_gate[expert_ids * cap + slot]
    return (grad_tokens, grad_gates)


def solution(mesh):
    placed = (
        P("ctx", "tp"),
        P("ctx", "tp"),
        P(("ctx", "tp"), None),
        P(("ctx", "tp"), None),
        P(("ctx", "tp"), None, None),
        P(("ctx", "tp"), None, None),
        P(("ctx", "tp"), None, None),
    )
    return jax.shard_map(
        body,
        mesh=mesh,
        in_specs=placed,
        out_specs=(P("ctx", "tp"), P(("ctx", "tp"), None)),
        check_vma=False,
    )
```

```python
import functools

import jax
import jax.numpy as jnp
from jax import lax
from jax.experimental import pallas as pl
from jax.experimental.pallas import tpu as pltpu
from jax.sharding import PartitionSpec as P

MESH = pl.DeviceIdType.MESH
F32 = jnp.float32
BF16 = jnp.bfloat16

CAP = 6
BLK = 48
CHUNK = 384
ROWS = 1536
TOK = 1024
SH = 512
HID = 768
WIDTH = 4096


def dot(left, right):
    return jnp.dot(left, right, preferred_element_type=F32)


def dot_last(left, right):
    return lax.dot_general(left, right, (((1,), (1,)), ((), ())), preferred_element_type=F32)


def kernel(
    pack, tok, dy, wg_hbm, wu_hbm, wd_hbm,
    out, vout,
    wg, wu, wd, xrow, yrow, stage, xg, dyz, yg, back, ret,
    pre, bh, posb, post, pgs, pgl, gs, gb,
    w_sem, pos_s, pos_r, z_s, z_r, a1_s, a1x_r, a1p_r, a2_s, a2_r,
    b2_s, b2_r, r1_s, r1_r, r2_s, r2_r, g1_s, g1_r, g2_s, g2_r,
):
    ctx, tp = lax.axis_index("ctx"), lax.axis_index("tp")
    zl, yc, x, zh = ctx // 8, ctx % 8, tp // 2, tp % 2
    ozl, ozh = 1 - zl, 1 - zh
    plane = zl * 2 + zh
    q = x * 8 + yc

    def dev(zl_, yc_, x_, zh_):
        return (zl_ * 8 + yc_, x_ * 2 + zh_)

    def plane_of(m):
        return (zl + ((m + 1) // 2) % 2) % 2, (zh + m // 2) % 2

    def peer(m):
        zl_, zh_ = plane_of(m)
        return dev(zl_, yc, x, zh_)

    def near_first(i):
        return i + (i // 2) * (5 - 2 * i)

    def rows(n):
        return pl.ds(pl.multiple_of(n * BLK, BLK), BLK)

    def chunk(n):
        return pl.ds(pl.multiple_of(n * CHUNK, CHUNK), CHUNK)

    def send(src, dst, s_sem, r_sem, to):
        pltpu.make_async_remote_copy(
            src_ref=src, dst_ref=dst, send_sem=s_sem, recv_sem=r_sem,
            device_id=to, device_id_type=MESH,
        ).start()

    def wait(ref, sem):
        pltpu.make_async_copy(ref, ref, sem).wait()

    bar = pltpu.get_barrier_semaphore()

    def greet_plane(i, c):
        to = dev(zl, (yc + i % 8) % 8, (x + i // 8) % 4, zh)
        pl.semaphore_signal(bar, inc=1, device_id=to, device_id_type=MESH)
        return c

    def greet_other(i, c):
        zl_, zh_ = plane_of(1 + i // 4)
        to = dev(zl_, yc, (x + i % 4) % 4, zh_)
        pl.semaphore_signal(bar, inc=1, device_id=to, device_id_type=MESH)
        return c

    lax.fori_loop(1, 32, greet_plane, 0)
    lax.fori_loop(0, 12, greet_other, 0)
    loads = [
        pltpu.make_async_copy(wg_hbm, wg, w_sem.at[0]),
        pltpu.make_async_copy(wu_hbm, wu, w_sem.at[1]),
        pltpu.make_async_copy(wd_hbm, wd, w_sem.at[2]),
    ]
    for load in loads:
        load.start()
    pl.semaphore_wait(bar, 43)

    mine = posb.at[zl * 8 + tp]
    pltpu.make_async_copy(pack, mine, pos_r).start()

    def send_pos(i, c):
        to = dev((zl + i // 8) % 2, yc, (x + (i // 2) % 4) % 4, (zh + i % 2) % 2)
        send(pack, mine, pos_s, pos_r, to)
        return c

    lax.fori_loop(1, 16, send_pos, 0)
    for m in (1, 2, 3):
        send(dy, dyz.at[m - 1], z_s.at[m - 1], z_r.at[m - 1], peer(m))
    wait(posb, pos_r)

    def select(zl_, c):
        place = (lax.broadcasted_iota(jnp.int32, (CHUNK, 128), 0) + c * CHUNK).astype(F32)
        parts = []
        for n in range(8):
            tile = posb[zl_ * 8 + n]
            hit = (place == tile[0:1]) | (place == tile[1:2])
            parts.append(jnp.where(hit, 1.0, 0.0).astype(BF16))
        return jnp.concatenate(parts, axis=1)

    def spread(i, src_of, dst_of, s_sem, r_sem, xd, dx):
        def one(j, c):
            ycd = (yc + j) % 8
            src, dst = src_of(rows(xd * 8 + ycd)), dst_of(rows(q))
            own = dx * 8 + j == 0

            @pl.when(own)
            def _():
                pltpu.make_async_copy(src, dst, r_sem).start()

            @pl.when(jnp.logical_not(own))
            def _():
                send(src, dst, s_sem, r_sem, dev(zl, ycd, xd, zh))

            return c

        lax.fori_loop(0, 8, one, 0)

    def x_out(i, c):
        dx = near_first(i)
        xd = (x + dx) % 4
        for s in (0, 1):
            zt = (zl + s) % 2
            xg[s, chunk(xd), :] = dot(select(zl, zt * 4 + xd), tok[...]).astype(BF16)
        spread(i, lambda r: xg.at[1, r], lambda r: stage.at[r], a1_s.at[1], a1p_r.at[dx], xd, dx)
        spread(i, lambda r: xg.at[0, r], lambda r: xrow.at[plane, r], a1_s.at[0], a1x_r.at[dx], xd, dx)
        return c

    def y_out(m):
        zl_, zh_ = plane_of(m)
        slot = m % 2
        src = dy if m == 0 else dyz.at[m - 1]
        if m > 0:
            wait(dyz.at[m - 1], z_r.at[m - 1])
        if m > 1:
            wait(yg.at[slot, pl.ds(0, ROWS - BLK)], b2_s.at[m - 2])
            old_zl, old_zh = plane_of(m - 2)
            wait(yrow.at[old_zl * 2 + old_zh, chunk(x)], b2_r.at[m - 2, 0])

        def step(i, c):
            dx = near_first(i)
            xd = (x + dx) % 4
            yg[slot, chunk(xd), :] = dot(select(zl_, zl * 4 + xd), src[...]).astype(BF16)
            spread(
                i, lambda r: yg.at[slot, r], lambda r: yrow.at[zl_ * 2 + zh_, r],
                b2_s.at[m], b2_r.at[m, dx], xd, dx,
            )
            return c

        lax.fori_loop(0, 4, step, 0)

    def forward(dx):
        part = chunk((x + 4 - dx) % 4)
        wait(stage.at[part], a1p_r.at[dx])
        for m in (1, 2):
            send(stage.at[part], xrow.at[plane, part], a2_s.at[m - 1], a2_r.at[m - 1, dx], peer(m))
        wait(xrow.at[plane, part], a1x_r.at[dx])
        send(xrow.at[plane, part], xrow.at[plane, part], a2_s.at[2], a2_r.at[2, dx], peer(3))

    lax.fori_loop(0, 4, x_out, 0)
    y_out(0)
    forward(0)
    forward(1)
    y_out(1)
    forward(3)
    y_out(2)
    forward(2)
    y_out(3)

    pre[...] = jnp.zeros_like(pre)
    bh[...] = jnp.zeros_like(bh)
    for load in loads:
        load.wait()

    def shard(n):
        return pl.ds(pl.multiple_of(n * SH, SH), SH)

    def consume(n, c):
        dx, m = near_first(n // 4), n % 4
        xs = (x + 4 - dx) % 4
        zl_, zh_ = plane_of(m)
        src = xrow.at[zl_ * 2 + zh_, chunk(xs)]

        @pl.when(m > 0)
        def _():
            wait(src, a2_r.at[m - 1, dx])

        part = shard(xs * 2 + zh_)
        pre[zl_] += dot(src[...], wg[part, :])
        pre[2 + zl_] += dot(src[...], wu[part, :])

        dx, m = near_first(n % 4), n // 4
        xs = (x + 4 - dx) % 4
        zl_, zh_ = plane_of(m)
        src = yrow.at[zl_ * 2 + zh_, chunk(xs)]

        @pl.when(jnp.logical_or(m > 1, dx > 0))
        def _():
            wait(src, b2_r.at[m, dx])

        bh[zl_] += dot_last(src[...], wd[:, shard(xs * 2 + zh_)])
        return c

    lax.fori_loop(0, 16, consume, 0)

    def inner(n, c):
        s, part = n // 8, rows(n % 8)
        av, bv, hv = pre[s, part, :], pre[2 + s, part, :], bh[s, part, :]
        sigma = 1.0 / (1.0 + jnp.exp(-av))
        active = av * sigma
        hidden = (active * bv).astype(BF16).astype(F32)
        wd[rows(n), 0:HID] = (hv * bv * sigma * (1.0 + av * (1.0 - sigma))).astype(BF16)
        wd[rows(n), HID : 2 * HID] = (hv * active).astype(BF16)
        gate = jnp.sum(hidden * hv, axis=1, keepdims=True)
        diag = lax.broadcasted_iota(jnp.int32, (BLK, 128), 0) == lax.broadcasted_iota(
            jnp.int32, (BLK, 128), 1
        )
        pgs[s, pl.ds(n % 8, 1), :] = jnp.sum(jnp.where(diag, gate, 0.0), axis=0, keepdims=True)
        return c

    lax.fori_loop(0, 16, inner, 0)
    for m in (1, 2, 3):
        send(pgs.at[plane_of(m)[0]], pgl.at[m - 1], g1_s.at[m - 1], g1_r.at[m - 1], peer(m))

    for m in (0, 1, 2):
        wait(xrow.at[0], a2_s.at[m])
    for s in (0, 1):
        wait(xg.at[s, pl.ds(0, ROWS - BLK)], a1_s.at[s])

    def x_back(i, c):
        dx = near_first(3 - i)
        xs = (x + dx) % 4
        part = chunk(xs)
        for m in (1, 2, 3, 0):
            zl_, zh_ = plane_of(m)
            piece = shard(xs * 2 + zh_)
            val = dot_last(wd[chunk(zl_), 0:HID], wg[piece, :])
            val += dot_last(wd[chunk(zl_), HID : 2 * HID], wu[piece, :])
            here = xrow.at[zl_ * 2 + zh_, part]
            here[...] = val.astype(BF16)
            if m > 0:
                send(here, back.at[m - 1, part], r1_s.at[m - 1], r1_r.at[m - 1, dx], peer(m))
        return c

    lax.fori_loop(0, 4, x_back, 0)

    for m in (1, 2, 3):
        wait(pgl.at[m - 1], g1_r.at[m - 1])
    gs[zl] = pgs[zl] + pgl[2]
    gs[ozl] = pgl[0] + pgl[1]
    pltpu.make_async_copy(gs, gb.at[q], g2_r).start()

    def send_gate(i, c):
        send(gs, gb.at[q], g2_s, g2_r, dev(zl, (yc + i % 8) % 8, (x + i // 8) % 4, zh))
        return c

    lax.fori_loop(1, 32, send_gate, 0)

    def pair_back(i, c):
        dx = near_first(3 - i)
        xs = (x + dx) % 4
        part = chunk(xs)
        for m in (1, 2, 3):
            wait(back.at[m - 1, part], r1_r.at[m - 1, dx])
        xg[0, part, :] = (
            xrow[plane, part, :].astype(F32) + back[2, part, :].astype(F32)
        ).astype(BF16)
        xg[1, part, :] = (
            back[0, part, :].astype(F32) + back[1, part, :].astype(F32)
        ).astype(BF16)
        for s in (0, 1):
            zt = (zl + s) % 2
            spread(
                i, lambda r: xg.at[s, r], lambda r: ret.at[zt, r],
                r2_s.at[s], r2_r.at[s, dx], xs, dx,
            )
        return c

    lax.fori_loop(0, 4, pair_back, 0)

    for n in range(8):
        post[pl.ds(n * 128, 128), :] = posb[zl * 8 + n].T
    post[pl.ds(TOK, 128), :] = jnp.full((128, 8), -1.0, F32)
    pre[0:3, :, 0:SH] = jnp.zeros((3, CHUNK, SH), F32)

    def combine(i, c):
        dx = near_first(3 - i)
        xs = (x + 4 - dx) % 4
        for s in (0, 1):
            zt = (zl + s) % 2
            src = ret.at[zt, chunk(xs)]
            wait(src, r2_r.at[s, dx])

            def part_of(n, c):
                tile = post[chunk(n), :]
                place = (
                    lax.broadcasted_iota(jnp.int32, (CHUNK, CHUNK), 1) + (zt * 4 + xs) * CHUNK
                ).astype(F32)
                weigh = jnp.where(place == tile[:, 0:1], tile[:, 2:3], 0.0) + jnp.where(
                    place == tile[:, 1:2], tile[:, 3:4], 0.0
                )
                pre[n, :, 0:SH] += dot(weigh.astype(BF16), src[...])
                return c

            lax.fori_loop(0, 3, part_of, 0)
        return c

    lax.fori_loop(0, 4, combine, 0)
    for n, size in enumerate((CHUNK, CHUNK, TOK - 2 * CHUNK)):
        out[pl.ds(n * CHUNK, size), :] = pre[n, 0:size, 0:SH].astype(BF16)

    wait(gb, g2_r)
    keep = lax.broadcasted_iota(jnp.int32, (32, 8, 128), 1) == yc
    for s in (0, 1):
        vout[s] = jnp.sum(jnp.where(keep, gb[:, s], 0.0), axis=1)

    wait(posb.at[pl.ds(0, 15)], pos_s)
    for m in (0, 1, 2):
        wait(dyz.at[m], z_s.at[m])
        wait(back.at[m], r1_s.at[m])
        wait(pgl.at[m], g1_s.at[m])
    for m in (2, 3):
        wait(yg.at[0, pl.ds(0, ROWS - BLK)], b2_s.at[m])
    for s in (0, 1):
        wait(xg.at[s, pl.ds(0, ROWS - BLK)], r2_s.at[s])
    wait(gb.at[pl.ds(0, 31)], g2_s)


def expert_layer(pack, tokens, grad_out, gate_w, up_w, down_w):
    vmem = pl.BlockSpec(memory_space=pltpu.VMEM)
    hbm = pl.BlockSpec(memory_space=pl.ANY)
    dma = pltpu.SemaphoreType.DMA
    return pl.pallas_call(
        kernel,
        name="expert_layer",
        out_shape=(
            jax.ShapeDtypeStruct((TOK, SH), BF16),
            jax.ShapeDtypeStruct((2, 32, 128), F32),
        ),
        in_specs=[vmem, vmem, vmem, hbm, hbm, hbm],
        out_specs=(vmem, vmem),
        scratch_shapes=[
            pltpu.VMEM((WIDTH, HID), BF16),
            pltpu.VMEM((WIDTH, HID), BF16),
            pltpu.VMEM((HID, WIDTH), BF16),
            pltpu.VMEM((4, ROWS, SH), BF16),
            pltpu.VMEM((4, ROWS, SH), BF16),
            pltpu.VMEM((ROWS, SH), BF16),
            pltpu.VMEM((2, ROWS, SH), BF16),
            pltpu.VMEM((3, TOK, SH), BF16),
            pltpu.VMEM((2, ROWS, SH), BF16),
            pltpu.VMEM((3, ROWS, SH), BF16),
            pltpu.VMEM((2, ROWS, SH), BF16),
            pltpu.VMEM((4, CHUNK, HID), F32),
            pltpu.VMEM((2, CHUNK, HID), F32),
            pltpu.VMEM((16, 8, 128), F32),
            pltpu.VMEM((3 * CHUNK, 8), F32),
            pltpu.VMEM((2, 8, 128), F32),
            pltpu.VMEM((3, 8, 128), F32),
            pltpu.VMEM((2, 8, 128), F32),
            pltpu.VMEM((32, 2, 8, 128), F32),
            dma((3,)),
            dma, dma,
            dma((3,)), dma((3,)),
            dma((2,)), dma((4,)), dma((4,)),
            dma((3,)), dma((3, 4)),
            dma((4,)), dma((4, 4)),
            dma((3,)), dma((3, 4)),
            dma((2,)), dma((2, 4)),
            dma((3,)), dma((3,)),
            dma, dma,
        ],
        compiler_params=pltpu.CompilerParams(
            collective_id=0, has_side_effects=True, vmem_limit_bytes=64 << 20
        ),
        cost_estimate=pl.CostEstimate(
            flops=36_000_000_000, bytes_accessed=25_000_000, transcendentals=600_000
        ),
    )(pack, tokens, grad_out, gate_w, up_w, down_w)


def body(tokens, grad_out, expert_ids, gates, w_gate, w_up, w_down):
    tok_rows, topk = expert_ids.shape
    experts = 64
    onehot = (expert_ids[:, :, None] == jnp.arange(experts, dtype=jnp.int32)).astype(F32)
    member = jnp.sum(onehot, axis=1)
    lower = (jnp.arange(tok_rows)[:, None] > jnp.arange(tok_rows)[None, :]).astype(F32)
    earlier = jnp.dot(lower, member)
    slot = jnp.sum(earlier[:, None, :] * onehot, axis=2).astype(jnp.int32)
    slot = slot + lax.axis_index("tp") * CAP
    half, yc, x = expert_ids // 32, expert_ids % 32 // 4, expert_ids % 4
    code = (half * 4 + x) * CHUNK + yc * BLK + slot
    pack = jnp.concatenate(
        [code.astype(F32).T, gates.T, jnp.zeros((4, tok_rows), F32)], axis=0
    )
    grad_tokens, terms = expert_layer(
        pack, tokens, grad_out, w_gate[0], w_up[0], w_down[0]
    )
    grad_gates = terms.reshape(-1)[(half * 32 + x * 8 + yc) * 128 + slot]
    return (grad_tokens, grad_gates)


def solution(mesh):
    placed = (
        P("ctx", "tp"),
        P("ctx", "tp"),
        P(("ctx", "tp"), None),
        P(("ctx", "tp"), None),
        P(("ctx", "tp"), None, None),
        P(("ctx", "tp"), None, None),
        P(("ctx", "tp"), None, None),
    )
    return jax.shard_map(
        body,
        mesh=mesh,
        in_specs=placed,
        out_specs=(P("ctx", "tp"), P(("ctx", "tp"), None)),
        check_vma=False,
    )
```

```python
import functools

import jax
import jax.numpy as jnp
from jax import lax
from jax.experimental import pallas as pl
from jax.experimental.pallas import tpu as pltpu
from jax.sharding import PartitionSpec as P

MESH = pl.DeviceIdType.MESH
FAR_FIRST = (
    (2, 2), (1, 2), (2, 1), (3, 2), (2, 3), (1, 1), (3, 3), (1, 3),
    (3, 1), (2, 0), (0, 2), (1, 0), (0, 1), (3, 0), (0, 3), (0, 0),
)
F32 = jnp.float32
BF16 = jnp.bfloat16

CAP = 6
BLK = 48
CHUNK = 384
ROWS = 1536
TOK = 1024
SH = 512
HID = 768
WIDTH = 4096
PART = 256


def dot(left, right):
    return jnp.dot(left, right, preferred_element_type=F32)


def dot_last(left, right):
    return lax.dot_general(left, right, (((1,), (1,)), ((), ())), preferred_element_type=F32)


def kernel(
    routes, tok, dy, wg_hbm, wu_hbm, wd_hbm,
    out, gate_out,
    wg, wu, wd, xrow, yrow, stage, buf, dyz, back, ret,
    pre, dab, pack, posb, post, pgs, pgl, gs, gb,
    w_sem, pos_s, pos_r, z_s, z_r, a1x_r, a1p_r, a2_s, a2_r,
    b_s, b2_r, r1_s, r1_r, r2_s, r2_r, p3_s, p3_r, g1_s, g1_r, g2_s, g2_r,
):
    ctx, tp = lax.axis_index("ctx"), lax.axis_index("tp")
    zl, yc, x, zh = ctx // 8, ctx % 8, tp // 2, tp % 2
    ozl = 1 - zl
    plane = zl * 2 + zh
    q = x * 8 + yc

    def dev(zl_, yc_, x_, zh_):
        return (zl_ * 8 + yc_, x_ * 2 + zh_)

    def plane_of(m):
        return (zl + ((m + 1) // 2) % 2) % 2, (zh + m // 2) % 2

    def place_of(m):
        zl_, zh_ = plane_of(m)
        return zl_ * 2 + zh_

    def peer(m):
        zl_, zh_ = plane_of(m)
        return dev(zl_, yc, x, zh_)

    def near_first(i):
        return i + (i // 2) * (5 - 2 * i)

    def rows(n):
        return pl.ds(pl.multiple_of(n * BLK, BLK), BLK)

    def chunk(n):
        return pl.ds(pl.multiple_of(n * CHUNK, CHUNK), CHUNK)

    def shard(n):
        return pl.ds(pl.multiple_of(n * SH, SH), SH)

    def send(src, dst, s_sem, r_sem, to):
        pltpu.make_async_remote_copy(
            src_ref=src, dst_ref=dst, send_sem=s_sem, recv_sem=r_sem,
            device_id=to, device_id_type=MESH,
        ).start()

    def wait(ref, sem):
        pltpu.make_async_copy(ref, ref, sem).wait()

    bar = pltpu.get_barrier_semaphore()

    def greet_plane(i, c):
        to = dev(zl, (yc + i % 8) % 8, (x + i // 8) % 4, zh)
        pl.semaphore_signal(bar, inc=1, device_id=to, device_id_type=MESH)
        return c

    def greet_other(i, c):
        zl_, zh_ = plane_of(1 + i // 4)
        to = dev(zl_, yc, (x + i % 4) % 4, zh_)
        pl.semaphore_signal(bar, inc=1, device_id=to, device_id_type=MESH)
        return c

    lax.fori_loop(0, 12, greet_other, 0)
    lax.fori_loop(1, 32, greet_plane, 0)
    loads = [
        pltpu.make_async_copy(wg_hbm, wg, w_sem.at[0]),
        pltpu.make_async_copy(wu_hbm, wu, w_sem.at[1]),
        pltpu.make_async_copy(wd_hbm, wd, w_sem.at[2]),
    ]
    for load in loads:
        load.start()

    ids = [routes[k : k + 1, :] for k in (0, 1)]
    expert = lax.broadcasted_iota(jnp.int32, (64, 128), 0).astype(F32)
    named = [jnp.where(expert == e, 1.0, 0.0) for e in ids]
    before = lax.broadcasted_iota(jnp.int32, (128, 128), 0) < lax.broadcasted_iota(
        jnp.int32, (128, 128), 1
    )
    earlier = dot((named[0] + named[1]).astype(BF16), jnp.where(before, 1.0, 0.0).astype(BF16))
    first = (tp * CAP).astype(F32)
    for k in (0, 1):
        slot = jnp.sum(named[k] * earlier, axis=0, keepdims=True) + first
        half = jnp.floor(ids[k] * (1 / 32))
        rest = ids[k] - half * 32.0
        line = jnp.floor(rest * 0.25)
        column = rest - line * 4.0
        pack[k : k + 1, :] = (half * 4.0 + column) * CHUNK + line * BLK + slot
        pack[2 + k : 3 + k, :] = routes[2 + k : 3 + k, :]
        pack[4 + k : 5 + k, :] = half * 32.0 + column * 8.0 + line
        pack[6 + k : 7 + k, :] = slot

    pl.semaphore_wait(bar, 43)

    top, low = pl.ds(0, TOK // 2), pl.ds(TOK // 2, TOK // 2)
    send(dy.at[top], dyz.at[0, top], z_s.at[0], z_r.at[0, 0], peer(1))
    send(dy.at[low], dyz.at[1, low], z_s.at[1], z_r.at[1, 1], peer(2))
    mine = posb.at[zl * 8 + tp]
    pltpu.make_async_copy(pack, mine, pos_r).start()

    def send_pos(i, c):
        to = dev((zl + i // 8) % 2, yc, (x + (i // 2) % 4) % 4, (zh + i % 2) % 2)
        send(pack, mine, pos_s, pos_r, to)
        return c

    lax.fori_loop(1, 16, send_pos, 0)
    wait(posb, pos_r)

    def select(zl_, c):
        place = (lax.broadcasted_iota(jnp.int32, (CHUNK, 128), 0) + c * CHUNK).astype(F32)
        parts = []
        for n in range(8):
            tile = posb[zl_ * 8 + n]
            hit = (place == tile[0:1]) | (place == tile[1:2])
            parts.append(jnp.where(hit, 1.0, 0.0).astype(BF16))
        return jnp.concatenate(parts, axis=1)

    def spread(src_of, dst, s_sem, r_sem_of):
        def side(n, c):
            dc = 1 - n
            for dx, dy in FAR_FIRST:
                xd, ycd = (x + dx) % 4, (yc // 2 + dy) % 4 * 2 + (yc + dc) % 2
                src = src_of(xd * 8 + ycd)
                go = functools.partial(
                    send, src, dst, s_sem, r_sem_of(dx), dev(zl, ycd, xd, zh)
                )
                if dx + dy > 0:
                    go()
                    continue

                @pl.when(dc == 0)
                def _():
                    pltpu.make_async_copy(src, dst, s_sem).start()

                pl.when(dc > 0)(go)
            return c

        lax.fori_loop(0, 2, side, 0)

    def arrived(ref, xs, sem, dx):
        @pl.when(dx > 0)
        def _():
            wait(ref.at[chunk(xs)], sem)

        @pl.when(dx == 0)
        def _():
            wait(ref.at[pl.ds(0, CHUNK - BLK)], sem)

    def left(b):
        wait(buf.at[pl.ds(0, ROWS)], b_s.at[b])

    def batch(b, slot, src, zl_src, zl_dst, dst, r_sem_of):
        def step(xd, c):
            picked = dot(select(zl_src, zl_dst * 4 + xd), src[...])
            buf[chunk(4 * slot + xd), :] = picked.astype(BF16)
            return c

        lax.fori_loop(0, 4, step, 0)
        spread(lambda k: buf.at[rows(32 * slot + k)], dst, b_s.at[b], r_sem_of)

    def x_out(b, slot, s):
        dst = stage.at[rows(q)] if s else xrow.at[plane, rows(q)]
        sem = a1p_r if s else a1x_r
        batch(b, slot, tok, zl, (zl + s) % 2, dst, lambda dx: sem.at[dx])

    def y_out(b, slot, m):
        src = dy if m == 0 else dyz.at[m - 1]
        dst = yrow.at[place_of(m), rows(q)]
        batch(b, slot, src, plane_of(m)[0], zl, dst, lambda dx: b2_r.at[m, dx])

    def forward_near(dx):
        xs = (x + 4 - dx) % 4
        part = chunk(xs)
        arrived(stage, xs, a1p_r.at[dx], dx)
        for m in (1, 2):
            send(stage.at[part], xrow.at[plane, part], a2_s.at[m - 1], a2_r.at[m - 1, dx], peer(m))

    def forward_far(dx):
        part = chunk((x + 4 - dx) % 4)
        send(xrow.at[plane, part], xrow.at[plane, part], a2_s.at[2], a2_r.at[2, dx], peer(3))

    def base_of(m):
        return 0 if m in (1, 2) else 3

    def take_x(m, dx):
        xs = (x + 4 - dx) % 4
        src = xrow.at[place_of(m), chunk(xs)]
        if m > 0:
            wait(src, a2_r.at[m - 1, dx])
        part = shard(xs * 2 + plane_of(m)[1])
        pre[base_of(m)] += dot(src[...], wg[part, :])
        pre[base_of(m) + 1] += dot(src[...], wu[part, :])

    def take_y(m, dx):
        xs = (x + 4 - dx) % 4
        arrived(yrow.at[place_of(m)], xs, b2_r.at[m, dx], dx)
        part = shard(xs * 2 + plane_of(m)[1])
        pre[base_of(m) + 2] += dot_last(yrow[place_of(m), chunk(xs), :], wd[:, part])

    def each(f):
        def step(i, c):
            f(near_first(i))
            return c

        lax.fori_loop(0, 4, step, 0)

    x_out(0, 0, 1)
    send(dy.at[low], dyz.at[0, low], z_s.at[0], z_r.at[0, 1], peer(1))
    send(dy.at[top], dyz.at[1, top], z_s.at[1], z_r.at[1, 0], peer(2))
    x_out(1, 1, 0)
    wait(dyz.at[0, top], z_r.at[0, 0])
    send(dyz.at[0, top], dyz.at[2, top], z_s.at[2], z_r.at[2, 0], peer(2))
    wait(dyz.at[1, low], z_r.at[1, 1])
    send(dyz.at[1, low], dyz.at[2, low], z_s.at[2], z_r.at[2, 1], peer(1))
    wait(dyz.at[0, low], z_r.at[0, 1])
    y_out(2, 2, 1)
    left(0)
    for dx in (0, 1, 3, 2):
        forward_near(dx)
    wait(dyz.at[1, top], z_r.at[1, 0])
    y_out(3, 0, 2)
    pre[...] = jnp.zeros_like(pre)
    for load in loads:
        load.wait()
    left(1)
    for dx in (0, 1, 3, 2):
        arrived(xrow.at[plane], (x + 4 - dx) % 4, a1x_r.at[dx], dx)
    each(lambda dx: take_x(0, dx))
    left(2)
    y_out(4, 2, 0)
    each(lambda dx: (take_x(1, dx), take_x(2, dx)))
    for m in (0, 1):
        wait(xrow.at[0], a2_s.at[m])
    for dx in (0, 1, 3, 2):
        forward_far(dx)
    wait(dyz.at[2, top], z_r.at[2, 0])
    wait(dyz.at[2, low], z_r.at[2, 1])
    left(3)
    y_out(5, 0, 3)
    each(lambda dx: take_y(1, dx))
    each(lambda dx: take_y(2, dx))

    def inner(g, dst):
        base = 0 if g else 3

        def step(n, c):
            part = rows(n)
            av, bv, hv = pre[base, part, :], pre[base + 1, part, :], pre[base + 2, part, :]
            sigma = 1.0 / (1.0 + jnp.exp(-av))
            active = av * sigma
            hidden = (active * bv).astype(BF16).astype(F32)
            dst[part, 0:HID] = (hv * bv * sigma * (1.0 + av * (1.0 - sigma))).astype(BF16)
            dst[part, HID : 2 * HID] = (hv * active).astype(BF16)
            gate = jnp.sum(hidden * hv, axis=1, keepdims=True)
            diag = lax.broadcasted_iota(jnp.int32, (BLK, 128), 0) == lax.broadcasted_iota(
                jnp.int32, (BLK, 128), 1
            )
            pgs[g, pl.ds(n, 1), :] = jnp.sum(jnp.where(diag, gate, 0.0), axis=0, keepdims=True)
            return c

        lax.fori_loop(0, 8, step, 0)

    def grad_x(src, m, xs):
        piece = shard(xs * 2 + plane_of(m)[1])
        val = dot_last(src[0:CHUNK, 0:HID], wg[piece, :])
        val += dot_last(src[0:CHUNK, HID : 2 * HID], wu[piece, :])
        here = xrow.at[place_of(m), chunk(xs)]
        here[...] = val.astype(BF16)
        return here

    inner(1, dab)
    for m in (1, 2):
        send(pgs.at[1], pgl.at[m - 1], g1_s.at[m - 1], g1_r.at[m - 1], peer(m))

    def back_near(dx):
        for m in (1, 2):
            grad_x(dab, m, (x + dx) % 4)

    each(back_near)
    left(4)
    each(lambda dx: take_y(0, dx))

    for n in range(8):
        post[pl.ds(n * 128, 128), :] = posb[zl * 8 + n].T

    def tokens_of(n):
        return pl.ds(pl.multiple_of(n * PART, PART), PART)

    def weigh(n, first, size):
        tile = post[tokens_of(n), :]
        place = (lax.broadcasted_iota(jnp.int32, (PART, size), 1) + first).astype(F32)
        hit = jnp.where(place == tile[:, 0:1], tile[:, 2:3], 0.0)
        return (hit + jnp.where(place == tile[:, 1:2], tile[:, 3:4], 0.0)).astype(BF16)

    wait(dyz.at[2], z_s.at[2])

    def weigh_own(n, c):
        for p in range(3):
            dyz[p, tokens_of(n), :] = weigh(n, zl * ROWS + p * SH, SH)
        return c

    lax.fori_loop(0, 4, weigh_own, 0)

    def total_own(n, k):
        total = dot(dyz[0, tokens_of(n), :], ret[k, 0:SH, :])
        for p in (1, 2):
            total += dot(dyz[p, tokens_of(n), :], ret[k, p * SH : (p + 1) * SH, :])
        return total

    wait(xrow.at[plane], a2_s.at[2])
    for i in (2, 3, 1, 0):
        part = chunk((x + i) % 4)
        for m in (1, 2):
            send(
                xrow.at[place_of(m), part], back.at[m - 1, part],
                r1_s.at[m - 1], r1_r.at[m - 1, i], peer(m),
            )

    each(lambda dx: take_x(3, dx))
    left(5)
    each(lambda dx: take_y(3, dx))
    inner(0, wd)
    send(pgs.at[0], pgl.at[2], g1_s.at[2], g1_r.at[2], peer(3))

    def back_own(m, k):
        each(lambda dx: grad_x(wd, m, dx))
        spread(
            lambda n: xrow.at[place_of(m), rows(n)], ret.at[k, rows(q)],
            r2_s.at[k], lambda dx: r2_r.at[k, dx],
        )

    back_own(3, 2)

    def pair_back():
        def step(dx):
            part = chunk((x + dx) % 4)
            for m in (1, 2):
                wait(back.at[m - 1, part], r1_r.at[m - 1, dx])
            pair = back[0, part, :].astype(F32) + back[1, part, :].astype(F32)
            buf[part, :] = pair.astype(BF16)

        each(step)
        spread(
            lambda n: buf.at[rows(n)], ret.at[0, rows(q)], r2_s.at[0],
            lambda dx: r2_r.at[0, dx],
        )

    wait(xrow.at[0], r2_s.at[2])
    back_own(0, 1)

    for dx in range(4):
        arrived(ret.at[2], (x + 4 - dx) % 4, r2_r.at[2, dx], dx)

    def far_total(n, c):
        here = pl.ds(pl.multiple_of(ROWS + n * PART, PART), PART)
        buf[here, :] = total_own(n, 2).astype(BF16)
        send(buf.at[here], out.at[tokens_of(n)], p3_s.at[n], p3_r.at[n], peer(3))
        return c

    lax.fori_loop(0, 4, far_total, 0)
    pair_back()

    for m in (1, 2, 3):
        wait(pgl.at[m - 1], g1_r.at[m - 1])
    gs[zl] = pgs[0] + pgl[2]
    gs[ozl] = pgl[0] + pgl[1]
    pltpu.make_async_copy(gs, gb.at[q], g2_r).start()

    def send_gate(i, c):
        send(gs, gb.at[q], g2_s, g2_r, dev(zl, (yc + i % 8) % 8, (x + i // 8) % 4, zh))
        return c

    lax.fori_loop(1, 32, send_gate, 0)

    wait(xrow.at[0], r2_s.at[1])
    for dx in range(4):
        arrived(ret.at[1], (x + 4 - dx) % 4, r2_r.at[1, dx], dx)

    def own_total(n, c):
        pre[n, 0:PART, 0:SH] = total_own(n, 1)
        return c

    lax.fori_loop(0, 4, own_total, 0)

    wait(gb, g2_r)
    keep = lax.broadcasted_iota(jnp.int32, (32, 8, 128), 1) == yc
    terms = jnp.concatenate([jnp.sum(jnp.where(keep, gb[:, s], 0.0), axis=1) for s in (0, 1)])
    terms = terms.T
    coarse = terms.astype(BF16)
    fine = (terms - coarse.astype(F32)).astype(BF16)
    lane = lax.broadcasted_iota(jnp.int32, (128, 128), 0).astype(F32)
    for k in (0, 1):
        at = jnp.where(expert == pack[4 + k : 5 + k, :], 1.0, 0.0).astype(BF16)
        found = dot(coarse, at) + dot(fine, at)
        gate_out[k : k + 1, :] = jnp.sum(
            jnp.where(lane == pack[6 + k : 7 + k, :], found, 0.0), axis=0, keepdims=True
        )

    wait(xrow.at[0], r2_s.at[0])

    def pair_total(dx):
        xs = (x + 4 - dx) % 4
        arrived(ret.at[0], xs, r2_r.at[0, dx], dx)

        def part_of(n, c):
            weights = weigh(n, (ozl * 4 + xs) * CHUNK, CHUNK)
            pre[n, 0:PART, 0:SH] += dot(weights, ret[0, chunk(xs), :])
            return c

        lax.fori_loop(0, 4, part_of, 0)

    lax.fori_loop(0, 4, lambda i, c: (pair_total(near_first(3 - i)), c)[1], 0)

    def finish(n, c):
        here = tokens_of(n)
        wait(out.at[here], p3_r.at[n])
        out[here, :] = (pre[n, 0:PART, 0:SH] + out[here, :].astype(F32)).astype(BF16)
        wait(out.at[here], p3_s.at[n])
        return c

    lax.fori_loop(0, 4, finish, 0)

    wait(posb.at[pl.ds(0, 15)], pos_s)
    for m in (0, 1, 2):
        wait(pgl.at[m], g1_s.at[m])
    for m in (0, 1):
        wait(dyz.at[m], z_s.at[m])
        wait(back.at[m], r1_s.at[m])
    wait(gb.at[pl.ds(0, 31)], g2_s)


def expert_layer(routes, tokens, grad_out, gate_w, up_w, down_w):
    vmem = pl.BlockSpec(memory_space=pltpu.VMEM)
    hbm = pl.BlockSpec(memory_space=pl.ANY)
    dma = pltpu.SemaphoreType.DMA
    return pl.pallas_call(
        kernel,
        name="expert_layer",
        out_shape=(
            jax.ShapeDtypeStruct((TOK, SH), BF16),
            jax.ShapeDtypeStruct((2, 128), F32),
        ),
        in_specs=[vmem, vmem, vmem, hbm, hbm, hbm],
        out_specs=(vmem, vmem),
        scratch_shapes=[
            pltpu.VMEM((WIDTH, HID), BF16),
            pltpu.VMEM((WIDTH, HID), BF16),
            pltpu.VMEM((HID, WIDTH), BF16),
            pltpu.VMEM((4, ROWS, SH), BF16),
            pltpu.VMEM((4, ROWS, SH), BF16),
            pltpu.VMEM((ROWS, SH), BF16),
            pltpu.VMEM((3 * ROWS, SH), BF16),
            pltpu.VMEM((3, TOK, SH), BF16),
            pltpu.VMEM((2, ROWS, SH), BF16),
            pltpu.VMEM((3, ROWS, SH), BF16),
            pltpu.VMEM((6, CHUNK, HID), F32),
            pltpu.VMEM((CHUNK, 2 * HID), BF16),
            pltpu.VMEM((8, 128), F32),
            pltpu.VMEM((16, 8, 128), F32),
            pltpu.VMEM((TOK, 8), F32),
            pltpu.VMEM((2, 8, 128), F32),
            pltpu.VMEM((3, 8, 128), F32),
            pltpu.VMEM((2, 8, 128), F32),
            pltpu.VMEM((32, 2, 8, 128), F32),
            dma((3,)),
            dma, dma,
            dma((3,)), dma((3, 2)),
            dma((4,)), dma((4,)),
            dma((3,)), dma((3, 4)),
            dma((6,)), dma((4, 4)),
            dma((2,)), dma((2, 4)),
            dma((3,)), dma((3, 4)),
            dma((4,)), dma((4,)),
            dma((3,)), dma((3,)),
            dma, dma,
        ],
        compiler_params=pltpu.CompilerParams(
            collective_id=0, has_side_effects=True, vmem_limit_bytes=64 << 20
        ),
        cost_estimate=pl.CostEstimate(
            flops=36_000_000_000, bytes_accessed=25_000_000, transcendentals=600_000
        ),
    )(routes, tokens, grad_out, gate_w, up_w, down_w)


def body(tokens, grad_out, expert_ids, gates, w_gate, w_up, w_down):
    tok_rows, topk = expert_ids.shape
    routes = jnp.concatenate([expert_ids.astype(F32), gates], axis=1).T
    grad_tokens, grad_gates = expert_layer(
        routes, tokens, grad_out, w_gate[0], w_up[0], w_down[0]
    )
    return (grad_tokens, grad_gates.T)


def solution(mesh):
    placed = (
        P("ctx", "tp"),
        P("ctx", "tp"),
        P(("ctx", "tp"), None),
        P(("ctx", "tp"), None),
        P(("ctx", "tp"), None, None),
        P(("ctx", "tp"), None, None),
        P(("ctx", "tp"), None, None),
    )
    return jax.shard_map(
        body,
        mesh=mesh,
        in_specs=placed,
        out_specs=(P("ctx", "tp"), P(("ctx", "tp"), None)),
        check_vma=False,
    )
```

```python
import functools

import jax
import jax.numpy as jnp
from jax import lax
from jax.experimental import pallas as pl
from jax.experimental.pallas import tpu as pltpu
from jax.sharding import PartitionSpec as P

MESH = pl.DeviceIdType.MESH
FAR_FIRST = (
    (2, 2), (1, 2), (2, 1), (3, 2), (2, 3), (1, 1), (3, 3), (1, 3),
    (3, 1), (2, 0), (0, 2), (1, 0), (0, 1), (3, 0), (0, 3), (0, 0),
)
F32 = jnp.float32
BF16 = jnp.bfloat16

CAP = 6
BLK = 48
CHUNK = 384
ROWS = 1536
TOK = 1024
SH = 512
HID = 768
WIDTH = 4096
PART = 256


def dot(left, right):
    return jnp.dot(left, right, preferred_element_type=F32)


def dot_last(left, right):
    return lax.dot_general(left, right, (((1,), (1,)), ((), ())), preferred_element_type=F32)


def kernel(
    names, gates, tok, dy, wg_hbm, wu_hbm, wd_hbm,
    out, gate_out,
    wg, wu, wd, xrow, yrow, stage, buf, dyz, back, ret,
    pre, dab, pack, posb, post, pgs, pgl, gs, gb,
    w_sem, pos_s, pos_r, z_s, z_r, a1x_r, a1p_r, a2_s, a2_r,
    b_s, b2_r, r1_s, r1_r, r2_s, r2_r, p3_s, p3_r, g1_s, g1_r, g2_s, g2_r,
):
    ctx, tp = lax.axis_index("ctx"), lax.axis_index("tp")
    zl, yc, x, zh = ctx // 8, ctx % 8, tp // 2, tp % 2
    ozl = 1 - zl
    plane = zl * 2 + zh
    q = x * 8 + yc

    def dev(zl_, yc_, x_, zh_):
        return (zl_ * 8 + yc_, x_ * 2 + zh_)

    def plane_of(m):
        return (zl + ((m + 1) // 2) % 2) % 2, (zh + m // 2) % 2

    def place_of(m):
        zl_, zh_ = plane_of(m)
        return zl_ * 2 + zh_

    def peer(m):
        zl_, zh_ = plane_of(m)
        return dev(zl_, yc, x, zh_)

    def near_first(i):
        return i + (i // 2) * (5 - 2 * i)

    def rows(n):
        return pl.ds(pl.multiple_of(n * BLK, BLK), BLK)

    def chunk(n):
        return pl.ds(pl.multiple_of(n * CHUNK, CHUNK), CHUNK)

    def shard(n):
        return pl.ds(pl.multiple_of(n * SH, SH), SH)

    def send(src, dst, s_sem, r_sem, to):
        pltpu.make_async_remote_copy(
            src_ref=src, dst_ref=dst, send_sem=s_sem, recv_sem=r_sem,
            device_id=to, device_id_type=MESH,
        ).start()

    def wait(ref, sem):
        pltpu.make_async_copy(ref, ref, sem).wait()

    bar = pltpu.get_barrier_semaphore()

    def greet_plane(i, c):
        to = dev(zl, (yc + i % 8) % 8, (x + i // 8) % 4, zh)
        pl.semaphore_signal(bar, inc=1, device_id=to, device_id_type=MESH)
        return c

    def greet_other(i, c):
        zl_, zh_ = plane_of(1 + i // 4)
        to = dev(zl_, yc, (x + i % 4) % 4, zh_)
        pl.semaphore_signal(bar, inc=1, device_id=to, device_id_type=MESH)
        return c

    lax.fori_loop(0, 12, greet_other, 0)
    lax.fori_loop(1, 32, greet_plane, 0)
    loads = [
        pltpu.make_async_copy(wg_hbm, wg, w_sem.at[0]),
        pltpu.make_async_copy(wu_hbm, wu, w_sem.at[1]),
        pltpu.make_async_copy(wd_hbm, wd, w_sem.at[2]),
    ]
    for load in loads:
        load.start()

    ids = [names[k : k + 1, :].astype(F32) for k in (0, 1)]
    expert = lax.broadcasted_iota(jnp.int32, (64, 128), 0).astype(F32)
    named = [jnp.where(expert == e, 1.0, 0.0) for e in ids]
    before = lax.broadcasted_iota(jnp.int32, (128, 128), 0) < lax.broadcasted_iota(
        jnp.int32, (128, 128), 1
    )
    earlier = dot((named[0] + named[1]).astype(BF16), jnp.where(before, 1.0, 0.0).astype(BF16))
    first = (tp * CAP).astype(F32)
    for k in (0, 1):
        slot = jnp.sum(named[k] * earlier, axis=0, keepdims=True) + first
        half = jnp.floor(ids[k] * (1 / 32))
        rest = ids[k] - half * 32.0
        line = jnp.floor(rest * 0.25)
        column = rest - line * 4.0
        pack[k : k + 1, :] = (half * 4.0 + column) * CHUNK + line * BLK + slot
        pack[2 + k : 3 + k, :] = gates[k : k + 1, :]
        pack[4 + k : 5 + k, :] = half * 32.0 + column * 8.0 + line
        pack[6 + k : 7 + k, :] = slot

    pl.semaphore_wait(bar, 43)

    top, low = pl.ds(0, TOK // 2), pl.ds(TOK // 2, TOK // 2)
    send(dy.at[top], dyz.at[0, top], z_s.at[0], z_r.at[0, 0], peer(1))
    send(dy.at[low], dyz.at[1, low], z_s.at[1], z_r.at[1, 1], peer(2))
    mine = posb.at[zl * 8 + tp]
    pltpu.make_async_copy(pack, mine, pos_r).start()

    def send_pos(i, c):
        to = dev((zl + i // 8) % 2, yc, (x + (i // 2) % 4) % 4, (zh + i % 2) % 2)
        send(pack, mine, pos_s, pos_r, to)
        return c

    lax.fori_loop(1, 16, send_pos, 0)
    wait(posb, pos_r)

    def select(zl_, c):
        place = (lax.broadcasted_iota(jnp.int32, (CHUNK, 128), 0) + c * CHUNK).astype(F32)
        parts = []
        for n in range(8):
            tile = posb[zl_ * 8 + n]
            hit = (place == tile[0:1]) | (place == tile[1:2])
            parts.append(jnp.where(hit, 1.0, 0.0).astype(BF16))
        return jnp.concatenate(parts, axis=1)

    def spread(src_of, dst, s_sem, r_sem_of):
        def side(n, c):
            dc = 1 - n
            for dx, dy in FAR_FIRST:
                xd, ycd = (x + dx) % 4, (yc // 2 + dy) % 4 * 2 + (yc + dc) % 2
                src = src_of(xd * 8 + ycd)
                go = functools.partial(
                    send, src, dst, s_sem, r_sem_of(dx), dev(zl, ycd, xd, zh)
                )
                if dx + dy > 0:
                    go()
                    continue

                @pl.when(dc == 0)
                def _():
                    pltpu.make_async_copy(src, dst, s_sem).start()

                pl.when(dc > 0)(go)
            return c

        lax.fori_loop(0, 2, side, 0)

    def spread_at(dx, src_of, dst, s_sem, r_sem):
        xd = (x + dx) % 4

        def one(j, c):
            ycd = (yc + j) % 8
            src = src_of(xd * 8 + ycd)
            own = dx * 8 + j == 0

            @pl.when(own)
            def _():
                pltpu.make_async_copy(src, dst, s_sem).start()

            @pl.when(jnp.logical_not(own))
            def _():
                send(src, dst, s_sem, r_sem, dev(zl, ycd, xd, zh))

            return c

        lax.fori_loop(0, 8, one, 0)

    def arrived(ref, xs, sem, dx):
        @pl.when(dx > 0)
        def _():
            wait(ref.at[chunk(xs)], sem)

        @pl.when(dx == 0)
        def _():
            wait(ref.at[pl.ds(0, CHUNK - BLK)], sem)

    def left(b):
        wait(buf.at[pl.ds(0, ROWS)], b_s.at[b])

    def batch(b, slot, src, zl_src, zl_dst, dst, r_sem_of):
        def step(i, c):
            dx = near_first(3 - i)
            xd = (x + dx) % 4
            picked = dot(select(zl_src, zl_dst * 4 + xd), src[...])
            buf[chunk(4 * slot + xd), :] = picked.astype(BF16)
            if b < 0:
                spread_at(dx, src_of, dst, b_s.at[b], r_sem_of(dx))
            return c

        def src_of(k):
            return buf.at[rows(32 * slot + k)]

        lax.fori_loop(0, 4, step, 0)
        if b >= 0:
            spread(src_of, dst, b_s.at[b], r_sem_of)

    def x_out(b, slot, s):
        dst = stage.at[rows(q)] if s else xrow.at[plane, rows(q)]
        sem = a1p_r if s else a1x_r
        batch(b, slot, tok, zl, (zl + s) % 2, dst, lambda dx: sem.at[dx])

    def y_out(b, slot, m):
        src = dy if m == 0 else dyz.at[m - 1]
        dst = yrow.at[place_of(m), rows(q)]
        batch(b, slot, src, plane_of(m)[0], zl, dst, lambda dx: b2_r.at[m, dx])

    def forward_near(dx):
        xs = (x + 4 - dx) % 4
        part = chunk(xs)
        arrived(stage, xs, a1p_r.at[dx], dx)
        for m in (1, 2):
            send(stage.at[part], xrow.at[plane, part], a2_s.at[m - 1], a2_r.at[m - 1, dx], peer(m))

    def forward_far(dx):
        part = chunk((x + 4 - dx) % 4)
        send(xrow.at[plane, part], xrow.at[plane, part], a2_s.at[2], a2_r.at[2, dx], peer(3))

    def base_of(m):
        return 0 if m in (1, 2) else 3

    def take_x(m, dx):
        xs = (x + 4 - dx) % 4
        src = xrow.at[place_of(m), chunk(xs)]
        if m > 0:
            wait(src, a2_r.at[m - 1, dx])
        part = shard(xs * 2 + plane_of(m)[1])
        pre[base_of(m)] += dot(src[...], wg[part, :])
        pre[base_of(m) + 1] += dot(src[...], wu[part, :])

    def take_y(m, dx):
        xs = (x + 4 - dx) % 4
        arrived(yrow.at[place_of(m)], xs, b2_r.at[m, dx], dx)
        part = shard(xs * 2 + plane_of(m)[1])
        pre[base_of(m) + 2] += dot_last(yrow[place_of(m), chunk(xs), :], wd[:, part])

    def each(f):
        def step(i, c):
            f(near_first(i))
            return c

        lax.fori_loop(0, 4, step, 0)

    x_out(0, 0, 1)
    send(dy.at[low], dyz.at[0, low], z_s.at[0], z_r.at[0, 1], peer(1))
    send(dy.at[top], dyz.at[1, top], z_s.at[1], z_r.at[1, 0], peer(2))
    x_out(1, 1, 0)
    wait(dyz.at[0, top], z_r.at[0, 0])
    send(dyz.at[0, top], dyz.at[2, top], z_s.at[2], z_r.at[2, 0], peer(2))
    wait(dyz.at[1, low], z_r.at[1, 1])
    send(dyz.at[1, low], dyz.at[2, low], z_s.at[2], z_r.at[2, 1], peer(1))
    wait(dyz.at[0, low], z_r.at[0, 1])
    y_out(2, 2, 1)
    left(0)
    for dx in (0, 1, 3, 2):
        forward_near(dx)
    wait(dyz.at[1, top], z_r.at[1, 0])
    y_out(3, 0, 2)
    pre[...] = jnp.zeros_like(pre)
    for load in loads:
        load.wait()
    left(1)
    for dx in (0, 1, 3, 2):
        arrived(xrow.at[plane], (x + 4 - dx) % 4, a1x_r.at[dx], dx)
    each(lambda dx: take_x(0, dx))
    left(2)
    y_out(4, 2, 0)
    each(lambda dx: (take_x(1, dx), take_x(2, dx)))
    for m in (0, 1):
        wait(xrow.at[0], a2_s.at[m])
    for dx in (0, 1, 3, 2):
        forward_far(dx)
    wait(dyz.at[2, top], z_r.at[2, 0])
    wait(dyz.at[2, low], z_r.at[2, 1])
    left(3)
    y_out(5, 0, 3)
    each(lambda dx: take_y(1, dx))
    each(lambda dx: take_y(2, dx))

    def inner(g, dst):
        base = 0 if g else 3

        def step(n, c):
            part = rows(n)
            av, bv, hv = pre[base, part, :], pre[base + 1, part, :], pre[base + 2, part, :]
            sigma = 1.0 / (1.0 + jnp.exp(-av))
            active = av * sigma
            hidden = (active * bv).astype(BF16).astype(F32)
            dst[part, 0:HID] = (hv * bv * sigma * (1.0 + av * (1.0 - sigma))).astype(BF16)
            dst[part, HID : 2 * HID] = (hv * active).astype(BF16)
            gate = jnp.sum(hidden * hv, axis=1, keepdims=True)
            diag = lax.broadcasted_iota(jnp.int32, (BLK, 128), 0) == lax.broadcasted_iota(
                jnp.int32, (BLK, 128), 1
            )
            pgs[g, pl.ds(n, 1), :] = jnp.sum(jnp.where(diag, gate, 0.0), axis=0, keepdims=True)
            return c

        lax.fori_loop(0, 8, step, 0)

    def grad_x(src, m, xs):
        piece = shard(xs * 2 + plane_of(m)[1])
        val = dot_last(src[0:CHUNK, 0:HID], wg[piece, :])
        val += dot_last(src[0:CHUNK, HID : 2 * HID], wu[piece, :])
        here = xrow.at[place_of(m), chunk(xs)]
        here[...] = val.astype(BF16)
        return here

    inner(1, dab)
    for m in (1, 2):
        send(pgs.at[1], pgl.at[m - 1], g1_s.at[m - 1], g1_r.at[m - 1], peer(m))

    def back_near(dx):
        for m in (1, 2):
            grad_x(dab, m, (x + dx) % 4)

    each(back_near)
    left(4)
    each(lambda dx: take_y(0, dx))

    for n in range(8):
        post[pl.ds(n * 128, 128), :] = posb[zl * 8 + n].T

    def tokens_of(n):
        return pl.ds(pl.multiple_of(n * PART, PART), PART)

    def weigh(n, first, size):
        tile = post[tokens_of(n), :]
        place = (lax.broadcasted_iota(jnp.int32, (PART, size), 1) + first).astype(F32)
        hit = jnp.where(place == tile[:, 0:1], tile[:, 2:3], 0.0)
        return (hit + jnp.where(place == tile[:, 1:2], tile[:, 3:4], 0.0)).astype(BF16)

    wait(dyz.at[2], z_s.at[2])

    def weigh_own(n, c):
        for p in range(3):
            dyz[p, tokens_of(n), :] = weigh(n, zl * ROWS + p * SH, SH)
        return c

    lax.fori_loop(0, 4, weigh_own, 0)

    def near_place(n, p):
        if p == 2:
            base = TOK + n % 2 * PART
            late = pl.ds(pl.multiple_of(base, PART), PART)
            return late, pl.ds(pl.multiple_of(2 * ROWS + base, PART), PART)
        base = n * PART
        if p == 1:
            return pl.ds(pl.multiple_of(base, PART), PART), None
        return None, pl.ds(pl.multiple_of(2 * ROWS + base, PART), PART)

    def weigh_near(n, c):
        first = ozl * ROWS
        buf[near_place(n, 0)[1], :] = weigh(n, first, SH)
        stage[near_place(n, 1)[0], :] = weigh(n, first + SH, SH)
        in_stage, in_buf = near_place(n, 2)
        tile = weigh(n, first + 2 * SH, SH)

        @pl.when(n < 2)
        def _():
            stage[in_stage, :] = tile

        @pl.when(n >= 2)
        def _():
            buf[in_buf, :] = tile

        return c

    def total_near(n):
        total = dot(buf[near_place(n, 0)[1], :], ret[0, 0:SH, :])
        total += dot(stage[near_place(n, 1)[0], :], ret[0, SH : 2 * SH, :])
        in_stage, in_buf = near_place(n, 2)
        last = jnp.where(n < 2, stage[in_stage, :], buf[in_buf, :])
        return total + dot(last, ret[0, 2 * SH : 3 * SH, :])


    def total_own(n, k):
        total = dot(dyz[0, tokens_of(n), :], ret[k, 0:SH, :])
        for p in (1, 2):
            total += dot(dyz[p, tokens_of(n), :], ret[k, p * SH : (p + 1) * SH, :])
        return total

    wait(xrow.at[plane], a2_s.at[2])
    for i in (2, 3, 1, 0):
        part = chunk((x + i) % 4)
        for m in (1, 2):
            send(
                xrow.at[place_of(m), part], back.at[m - 1, part],
                r1_s.at[m - 1], r1_r.at[m - 1, i], peer(m),
            )

    lax.fori_loop(0, 4, weigh_near, 0)

    each(lambda dx: take_x(3, dx))
    left(5)
    each(lambda dx: take_y(3, dx))
    inner(0, wd)
    send(pgs.at[0], pgl.at[2], g1_s.at[2], g1_r.at[2], peer(3))

    def back_own(m, k, at_once):
        def src_of(n):
            return xrow.at[place_of(m), rows(n)]

        def step(i, c):
            dx = near_first(3 - i)
            grad_x(wd, m, (x + dx) % 4)
            if at_once:
                spread_at(dx, src_of, ret.at[k, rows(q)], r2_s.at[k], r2_r.at[k, dx])
            return c

        lax.fori_loop(0, 4, step, 0)
        if not at_once:
            spread(src_of, ret.at[k, rows(q)], r2_s.at[k], lambda dx: r2_r.at[k, dx])

    back_own(3, 2, False)
    back_own(0, 1, False)

    def pair_back():
        def step(dx):
            part = chunk((x + dx) % 4)
            for m in (1, 2):
                wait(back.at[m - 1, part], r1_r.at[m - 1, dx])
            pair = back[0, part, :].astype(F32) + back[1, part, :].astype(F32)
            buf[part, :] = pair.astype(BF16)

        each(step)
        spread(
            lambda n: buf.at[rows(n)], ret.at[0, rows(q)], r2_s.at[0],
            lambda dx: r2_r.at[0, dx],
        )

    wait(xrow.at[0], r2_s.at[2])
    for dx in range(4):
        arrived(ret.at[2], (x + 4 - dx) % 4, r2_r.at[2, dx], dx)

    def far_total(n, c):
        here = pl.ds(pl.multiple_of(ROWS + n * PART, PART), PART)
        buf[here, :] = total_own(n, 2).astype(BF16)
        send(buf.at[here], out.at[tokens_of(n)], p3_s.at[n], p3_r.at[n], peer(3))
        return c

    lax.fori_loop(0, 4, far_total, 0)
    pair_back()

    for m in (1, 2, 3):
        wait(pgl.at[m - 1], g1_r.at[m - 1])
    gs[zl] = pgs[0] + pgl[2]
    gs[ozl] = pgl[0] + pgl[1]
    pltpu.make_async_copy(gs, gb.at[q], g2_r).start()

    def send_gate(i, c):
        send(gs, gb.at[q], g2_s, g2_r, dev(zl, (yc + i % 8) % 8, (x + i // 8) % 4, zh))
        return c

    lax.fori_loop(1, 32, send_gate, 0)

    wait(xrow.at[0], r2_s.at[1])
    for dx in range(4):
        arrived(ret.at[1], (x + 4 - dx) % 4, r2_r.at[1, dx], dx)

    def own_total(n, c):
        pre[n, 0:PART, 0:SH] = total_own(n, 1)
        return c

    lax.fori_loop(0, 4, own_total, 0)

    wait(gb, g2_r)
    keep = lax.broadcasted_iota(jnp.int32, (32, 8, 128), 1) == yc
    terms = jnp.concatenate([jnp.sum(jnp.where(keep, gb[:, s], 0.0), axis=1) for s in (0, 1)])
    terms = terms.T
    coarse = terms.astype(BF16)
    fine = (terms - coarse.astype(F32)).astype(BF16)
    lane = lax.broadcasted_iota(jnp.int32, (128, 128), 0).astype(F32)
    for k in (0, 1):
        at = jnp.where(expert == pack[4 + k : 5 + k, :], 1.0, 0.0).astype(BF16)
        found = dot(coarse, at) + dot(fine, at)
        gate_out[k : k + 1, :] = jnp.sum(
            jnp.where(lane == pack[6 + k : 7 + k, :], found, 0.0), axis=0, keepdims=True
        )

    wait(xrow.at[0], r2_s.at[0])

    for dx in range(4):
        arrived(ret.at[0], (x + 4 - dx) % 4, r2_r.at[0, dx], dx)

    def finish(n, c):
        here = tokens_of(n)
        total = pre[n, 0:PART, 0:SH] + total_near(n)
        wait(out.at[here], p3_r.at[n])
        out[here, :] = (total + out[here, :].astype(F32)).astype(BF16)
        wait(out.at[here], p3_s.at[n])
        return c

    lax.fori_loop(0, 4, finish, 0)

    wait(posb.at[pl.ds(0, 15)], pos_s)
    for m in (0, 1, 2):
        wait(pgl.at[m], g1_s.at[m])
    for m in (0, 1):
        wait(dyz.at[m], z_s.at[m])
        wait(back.at[m], r1_s.at[m])
    wait(gb.at[pl.ds(0, 31)], g2_s)


def expert_layer(names, gates, tokens, grad_out, gate_w, up_w, down_w):
    vmem = pl.BlockSpec(memory_space=pltpu.VMEM)
    hbm = pl.BlockSpec(memory_space=pl.ANY)
    dma = pltpu.SemaphoreType.DMA
    return pl.pallas_call(
        kernel,
        name="expert_layer",
        out_shape=(
            jax.ShapeDtypeStruct((TOK, SH), BF16),
            jax.ShapeDtypeStruct((2, 128), F32),
        ),
        in_specs=[vmem, vmem, vmem, vmem, hbm, hbm, hbm],
        out_specs=(vmem, vmem),
        scratch_shapes=[
            pltpu.VMEM((WIDTH, HID), BF16),
            pltpu.VMEM((WIDTH, HID), BF16),
            pltpu.VMEM((HID, WIDTH), BF16),
            pltpu.VMEM((4, ROWS, SH), BF16),
            pltpu.VMEM((4, ROWS, SH), BF16),
            pltpu.VMEM((ROWS, SH), BF16),
            pltpu.VMEM((3 * ROWS, SH), BF16),
            pltpu.VMEM((3, TOK, SH), BF16),
            pltpu.VMEM((2, ROWS, SH), BF16),
            pltpu.VMEM((3, ROWS, SH), BF16),
            pltpu.VMEM((6, CHUNK, HID), F32),
            pltpu.VMEM((CHUNK, 2 * HID), BF16),
            pltpu.VMEM((8, 128), F32),
            pltpu.VMEM((16, 8, 128), F32),
            pltpu.VMEM((TOK, 8), F32),
            pltpu.VMEM((2, 8, 128), F32),
            pltpu.VMEM((3, 8, 128), F32),
            pltpu.VMEM((2, 8, 128), F32),
            pltpu.VMEM((32, 2, 8, 128), F32),
            dma((3,)),
            dma, dma,
            dma((3,)), dma((3, 2)),
            dma((4,)), dma((4,)),
            dma((3,)), dma((3, 4)),
            dma((6,)), dma((4, 4)),
            dma((2,)), dma((2, 4)),
            dma((3,)), dma((3, 4)),
            dma((4,)), dma((4,)),
            dma((3,)), dma((3,)),
            dma, dma,
        ],
        compiler_params=pltpu.CompilerParams(
            collective_id=0, has_side_effects=True, vmem_limit_bytes=64 << 20
        ),
        cost_estimate=pl.CostEstimate(
            flops=36_000_000_000, bytes_accessed=25_000_000, transcendentals=600_000
        ),
    )(names, gates, tokens, grad_out, gate_w, up_w, down_w)


def body(tokens, grad_out, expert_ids, gates, w_gate, w_up, w_down):
    grad_tokens, grad_gates = expert_layer(
        expert_ids.T, gates.T, tokens, grad_out, w_gate[0], w_up[0], w_down[0]
    )
    return (grad_tokens, grad_gates.T)


def solution(mesh):
    placed = (
        P("ctx", "tp"),
        P("ctx", "tp"),
        P(("ctx", "tp"), None),
        P(("ctx", "tp"), None),
        P(("ctx", "tp"), None, None),
        P(("ctx", "tp"), None, None),
        P(("ctx", "tp"), None, None),
    )
    return jax.shard_map(
        body,
        mesh=mesh,
        in_specs=placed,
        out_specs=(P("ctx", "tp"), P(("ctx", "tp"), None)),
        check_vma=False,
    )
```

```python
import functools

import jax
import jax.numpy as jnp
from jax import lax
from jax.experimental import pallas as pl
from jax.experimental.pallas import tpu as pltpu
from jax.sharding import PartitionSpec as P

MESH = pl.DeviceIdType.MESH
STEPS = (
    (2, 2), (1, 0), (0, 1), (2, 1), (3, 0), (0, 3), (1, 2), (2, 3),
    (3, 2), (1, 1), (3, 3), (2, 0), (0, 2), (1, 3), (3, 1), (0, 0),
)
F32 = jnp.float32
BF16 = jnp.bfloat16

CAP = 6
BLK = 48
CHUNK = 384
ROWS = 1536
TOK = 1024
SH = 512
HID = 768
WIDTH = 4096
PART = 256


def dot(left, right):
    return jnp.dot(left, right, preferred_element_type=F32)


def dot_last(left, right):
    return lax.dot_general(left, right, (((1,), (1,)), ((), ())), preferred_element_type=F32)


def kernel(
    names, gates, tok, dy, wg_hbm, wu_hbm, wd_hbm,
    out, gate_out,
    wg, wu, wd, xrow, yrow, stage, buf, dyz, back, ret,
    pre, dab, pack, posb, post, pgs, pgl, gs, gb,
    w_sem, pos_s, pos_r, z_s, z_r, a1x_r, a1p_r, a2_s, a2_r,
    b_s, b2_r, r1_s, r1_r, r2_s, r2_r, p3_s, p3_r, g1_s, g1_r, g2_s, g2_r,
):
    ctx, tp = lax.axis_index("ctx"), lax.axis_index("tp")
    zl, yc, x, zh = ctx // 8, ctx % 8, tp // 2, tp % 2
    ozl = 1 - zl
    plane = zl * 2 + zh
    q = x * 8 + yc

    def dev(zl_, yc_, x_, zh_):
        return (zl_ * 8 + yc_, x_ * 2 + zh_)

    def plane_of(m):
        return (zl + ((m + 1) // 2) % 2) % 2, (zh + m // 2) % 2

    def place_of(m):
        zl_, zh_ = plane_of(m)
        return zl_ * 2 + zh_

    def peer(m):
        zl_, zh_ = plane_of(m)
        return dev(zl_, yc, x, zh_)

    def near_first(i):
        return i + (i // 2) * (5 - 2 * i)

    def rows(n):
        return pl.ds(pl.multiple_of(n * BLK, BLK), BLK)

    def chunk(n):
        return pl.ds(pl.multiple_of(n * CHUNK, CHUNK), CHUNK)

    def shard(n):
        return pl.ds(pl.multiple_of(n * SH, SH), SH)

    def send(src, dst, s_sem, r_sem, to):
        pltpu.make_async_remote_copy(
            src_ref=src, dst_ref=dst, send_sem=s_sem, recv_sem=r_sem,
            device_id=to, device_id_type=MESH,
        ).start()

    def wait(ref, sem):
        pltpu.make_async_copy(ref, ref, sem).wait()

    bar = pltpu.get_barrier_semaphore()

    def greet_plane(i, c):
        to = dev(zl, (yc + i % 8) % 8, (x + i // 8) % 4, zh)
        pl.semaphore_signal(bar, inc=1, device_id=to, device_id_type=MESH)
        return c

    def greet_other(i, c):
        zl_, zh_ = plane_of(1 + i // 4)
        to = dev(zl_, yc, (x + i % 4) % 4, zh_)
        pl.semaphore_signal(bar, inc=1, device_id=to, device_id_type=MESH)
        return c

    lax.fori_loop(0, 12, greet_other, 0)
    lax.fori_loop(1, 32, greet_plane, 0)
    loads = [
        pltpu.make_async_copy(wg_hbm, wg, w_sem.at[0]),
        pltpu.make_async_copy(wu_hbm, wu, w_sem.at[1]),
        pltpu.make_async_copy(wd_hbm, wd, w_sem.at[2]),
    ]
    for load in loads:
        load.start()

    ids = [names[k : k + 1, :].astype(F32) for k in (0, 1)]
    expert = lax.broadcasted_iota(jnp.int32, (64, 128), 0).astype(F32)
    named = [jnp.where(expert == e, 1.0, 0.0) for e in ids]
    before = lax.broadcasted_iota(jnp.int32, (128, 128), 0) < lax.broadcasted_iota(
        jnp.int32, (128, 128), 1
    )
    earlier = dot((named[0] + named[1]).astype(BF16), jnp.where(before, 1.0, 0.0).astype(BF16))
    first = (tp * CAP).astype(F32)
    for k in (0, 1):
        slot = jnp.sum(named[k] * earlier, axis=0, keepdims=True) + first
        half = jnp.floor(ids[k] * (1 / 32))
        rest = ids[k] - half * 32.0
        line = jnp.floor(rest * 0.25)
        column = rest - line * 4.0
        pack[k : k + 1, :] = (half * 4.0 + column) * CHUNK + line * BLK + slot
        pack[2 + k : 3 + k, :] = gates[k : k + 1, :]
        pack[4 + k : 5 + k, :] = half * 32.0 + column * 8.0 + line
        pack[6 + k : 7 + k, :] = slot

    pl.semaphore_wait(bar, 43)

    top, low = pl.ds(0, TOK // 2), pl.ds(TOK // 2, TOK // 2)
    send(dy.at[top], dyz.at[0, top], z_s.at[0], z_r.at[0, 0], peer(1))
    send(dy.at[low], dyz.at[1, low], z_s.at[1], z_r.at[1, 1], peer(2))
    mine = posb.at[zl * 8 + tp]
    pltpu.make_async_copy(pack, mine, pos_r).start()

    def send_pos(i, c):
        to = dev((zl + i // 8) % 2, yc, (x + (i // 2) % 4) % 4, (zh + i % 2) % 2)
        send(pack, mine, pos_s, pos_r, to)
        return c

    lax.fori_loop(1, 16, send_pos, 0)
    wait(posb, pos_r)

    def select(zl_, c):
        place = (lax.broadcasted_iota(jnp.int32, (CHUNK, 128), 0) + c * CHUNK).astype(F32)
        parts = []
        for n in range(8):
            tile = posb[zl_ * 8 + n]
            hit = (place == tile[0:1]) | (place == tile[1:2])
            parts.append(jnp.where(hit, 1.0, 0.0).astype(BF16))
        return jnp.concatenate(parts, axis=1)

    def spread(src_of, dst, s_sem, r_sem_of):
        def side(n, c):
            dc = 1 - n
            for dx, dy in STEPS:
                xd, ycd = (x + dx) % 4, (yc // 2 + dy) % 4 * 2 + (yc + dc) % 2
                src = src_of(xd * 8 + ycd)
                go = functools.partial(
                    send, src, dst, s_sem, r_sem_of(dx), dev(zl, ycd, xd, zh)
                )
                if dx + dy > 0:
                    go()
                    continue

                @pl.when(dc == 0)
                def _():
                    pltpu.make_async_copy(src, dst, s_sem).start()

                pl.when(dc > 0)(go)
            return c

        lax.fori_loop(0, 2, side, 0)

    def spread_at(dx, src_of, dst, s_sem, r_sem):
        xd = (x + dx) % 4

        def one(j, c):
            ycd = (yc + j) % 8
            src = src_of(xd * 8 + ycd)
            own = dx * 8 + j == 0

            @pl.when(own)
            def _():
                pltpu.make_async_copy(src, dst, s_sem).start()

            @pl.when(jnp.logical_not(own))
            def _():
                send(src, dst, s_sem, r_sem, dev(zl, ycd, xd, zh))

            return c

        lax.fori_loop(0, 8, one, 0)

    def arrived(ref, xs, sem, dx):
        @pl.when(dx > 0)
        def _():
            wait(ref.at[chunk(xs)], sem)

        @pl.when(dx == 0)
        def _():
            wait(ref.at[pl.ds(0, CHUNK - BLK)], sem)

    def left(b):
        wait(buf.at[pl.ds(0, ROWS)], b_s.at[b])

    def batch(b, slot, src, zl_src, zl_dst, dst, r_sem_of):
        def step(i, c):
            dx = near_first(3 - i)
            xd = (x + dx) % 4
            picked = dot(select(zl_src, zl_dst * 4 + xd), src[...])
            buf[chunk(4 * slot + xd), :] = picked.astype(BF16)
            if b < 0:
                spread_at(dx, src_of, dst, b_s.at[b], r_sem_of(dx))
            return c

        def src_of(k):
            return buf.at[rows(32 * slot + k)]

        lax.fori_loop(0, 4, step, 0)
        if b >= 0:
            spread(src_of, dst, b_s.at[b], r_sem_of)

    def x_out(b, slot, s):
        dst = stage.at[rows(q)] if s else xrow.at[plane, rows(q)]
        sem = a1p_r if s else a1x_r
        batch(b, slot, tok, zl, (zl + s) % 2, dst, lambda dx: sem.at[dx])

    def y_out(b, slot, m):
        src = dy if m == 0 else dyz.at[m - 1]
        dst = yrow.at[place_of(m), rows(q)]
        batch(b, slot, src, plane_of(m)[0], zl, dst, lambda dx: b2_r.at[m, dx])

    def forward_near(dx):
        xs = (x + 4 - dx) % 4
        part = chunk(xs)
        arrived(stage, xs, a1p_r.at[dx], dx)
        for m in (1, 2):
            send(stage.at[part], xrow.at[plane, part], a2_s.at[m - 1], a2_r.at[m - 1, dx], peer(m))

    def forward_far(dx):
        part = chunk((x + 4 - dx) % 4)
        send(xrow.at[plane, part], xrow.at[plane, part], a2_s.at[2], a2_r.at[2, dx], peer(3))

    def base_of(m):
        return 0 if m in (1, 2) else 3

    def take_x(m, dx):
        xs = (x + 4 - dx) % 4
        src = xrow.at[place_of(m), chunk(xs)]
        if m > 0:
            wait(src, a2_r.at[m - 1, dx])
        part = shard(xs * 2 + plane_of(m)[1])
        pre[base_of(m)] += dot(src[...], wg[part, :])
        pre[base_of(m) + 1] += dot(src[...], wu[part, :])

    def take_y(m, dx):
        xs = (x + 4 - dx) % 4
        arrived(yrow.at[place_of(m)], xs, b2_r.at[m, dx], dx)
        part = shard(xs * 2 + plane_of(m)[1])
        pre[base_of(m) + 2] += dot_last(yrow[place_of(m), chunk(xs), :], wd[:, part])

    def each(f):
        def step(i, c):
            f(near_first(i))
            return c

        lax.fori_loop(0, 4, step, 0)

    x_out(0, 0, 1)
    send(dy.at[low], dyz.at[0, low], z_s.at[0], z_r.at[0, 1], peer(1))
    send(dy.at[top], dyz.at[1, top], z_s.at[1], z_r.at[1, 0], peer(2))
    x_out(1, 1, 0)
    wait(dyz.at[0, top], z_r.at[0, 0])
    send(dyz.at[0, top], dyz.at[2, top], z_s.at[2], z_r.at[2, 0], peer(2))
    wait(dyz.at[1, low], z_r.at[1, 1])
    send(dyz.at[1, low], dyz.at[2, low], z_s.at[2], z_r.at[2, 1], peer(1))
    wait(dyz.at[0, low], z_r.at[0, 1])
    y_out(2, 2, 1)
    left(0)
    for dx in (0, 1, 3, 2):
        forward_near(dx)
    wait(dyz.at[1, top], z_r.at[1, 0])
    y_out(3, 0, 2)
    pre[...] = jnp.zeros_like(pre)
    for load in loads:
        load.wait()
    left(1)
    for dx in (0, 1, 3, 2):
        arrived(xrow.at[plane], (x + 4 - dx) % 4, a1x_r.at[dx], dx)
    each(lambda dx: take_x(0, dx))
    left(2)
    y_out(4, 2, 0)
    each(lambda dx: (take_x(1, dx), take_x(2, dx)))
    for m in (0, 1):
        wait(xrow.at[0], a2_s.at[m])
    for dx in (0, 1, 3, 2):
        forward_far(dx)
    wait(dyz.at[2, top], z_r.at[2, 0])
    wait(dyz.at[2, low], z_r.at[2, 1])
    left(3)
    y_out(5, 0, 3)
    each(lambda dx: take_y(1, dx))
    each(lambda dx: take_y(2, dx))

    def inner(g, dst):
        base = 0 if g else 3

        def step(n, c):
            part = rows(n)
            av, bv, hv = pre[base, part, :], pre[base + 1, part, :], pre[base + 2, part, :]
            sigma = 1.0 / (1.0 + jnp.exp(-av))
            active = av * sigma
            hidden = (active * bv).astype(BF16).astype(F32)
            dst[part, 0:HID] = (hv * bv * sigma * (1.0 + av * (1.0 - sigma))).astype(BF16)
            dst[part, HID : 2 * HID] = (hv * active).astype(BF16)
            gate = jnp.sum(hidden * hv, axis=1, keepdims=True)
            diag = lax.broadcasted_iota(jnp.int32, (BLK, 128), 0) == lax.broadcasted_iota(
                jnp.int32, (BLK, 128), 1
            )
            pgs[g, pl.ds(n, 1), :] = jnp.sum(jnp.where(diag, gate, 0.0), axis=0, keepdims=True)
            return c

        lax.fori_loop(0, 8, step, 0)

    def grad_x(src, m, xs):
        piece = shard(xs * 2 + plane_of(m)[1])
        val = dot_last(src[0:CHUNK, 0:HID], wg[piece, :])
        val += dot_last(src[0:CHUNK, HID : 2 * HID], wu[piece, :])
        here = xrow.at[place_of(m), chunk(xs)]
        here[...] = val.astype(BF16)
        return here

    inner(1, dab)
    for m in (1, 2):
        send(pgs.at[1], pgl.at[m - 1], g1_s.at[m - 1], g1_r.at[m - 1], peer(m))

    def back_near(dx):
        for m in (1, 2):
            grad_x(dab, m, (x + dx) % 4)

    each(back_near)
    left(4)
    each(lambda dx: take_y(0, dx))

    for n in range(8):
        post[pl.ds(n * 128, 128), :] = posb[zl * 8 + n].T

    def tokens_of(n):
        return pl.ds(pl.multiple_of(n * PART, PART), PART)

    def weigh(n, first, size):
        tile = post[tokens_of(n), :]
        place = (lax.broadcasted_iota(jnp.int32, (PART, size), 1) + first).astype(F32)
        hit = jnp.where(place == tile[:, 0:1], tile[:, 2:3], 0.0)
        return (hit + jnp.where(place == tile[:, 1:2], tile[:, 3:4], 0.0)).astype(BF16)

    wait(dyz.at[2], z_s.at[2])

    def weigh_own(n, c):
        for p in range(3):
            dyz[p, tokens_of(n), :] = weigh(n, zl * ROWS + p * SH, SH)
        return c

    lax.fori_loop(0, 4, weigh_own, 0)

    def near_place(n, p):
        if p == 2:
            base = TOK + n % 2 * PART
            late = pl.ds(pl.multiple_of(base, PART), PART)
            return late, pl.ds(pl.multiple_of(2 * ROWS + base, PART), PART)
        base = n * PART
        if p == 1:
            return pl.ds(pl.multiple_of(base, PART), PART), None
        return None, pl.ds(pl.multiple_of(2 * ROWS + base, PART), PART)

    def weigh_near(n, c):
        first = ozl * ROWS
        buf[near_place(n, 0)[1], :] = weigh(n, first, SH)
        stage[near_place(n, 1)[0], :] = weigh(n, first + SH, SH)
        in_stage, in_buf = near_place(n, 2)
        tile = weigh(n, first + 2 * SH, SH)

        @pl.when(n < 2)
        def _():
            stage[in_stage, :] = tile

        @pl.when(n >= 2)
        def _():
            buf[in_buf, :] = tile

        return c

    def total_near(n):
        total = dot(buf[near_place(n, 0)[1], :], ret[0, 0:SH, :])
        total += dot(stage[near_place(n, 1)[0], :], ret[0, SH : 2 * SH, :])
        in_stage, in_buf = near_place(n, 2)
        last = jnp.where(n < 2, stage[in_stage, :], buf[in_buf, :])
        return total + dot(last, ret[0, 2 * SH : 3 * SH, :])


    def total_own(n, k):
        total = dot(dyz[0, tokens_of(n), :], ret[k, 0:SH, :])
        for p in (1, 2):
            total += dot(dyz[p, tokens_of(n), :], ret[k, p * SH : (p + 1) * SH, :])
        return total

    wait(xrow.at[plane], a2_s.at[2])
    for i in (2, 3, 1, 0):
        part = chunk((x + i) % 4)
        for m in (1, 2):
            send(
                xrow.at[place_of(m), part], back.at[m - 1, part],
                r1_s.at[m - 1], r1_r.at[m - 1, i], peer(m),
            )

    lax.fori_loop(0, 4, weigh_near, 0)

    each(lambda dx: take_x(3, dx))
    left(5)
    each(lambda dx: take_y(3, dx))
    inner(0, wd)
    send(pgs.at[0], pgl.at[2], g1_s.at[2], g1_r.at[2], peer(3))

    def back_own(m, k, at_once):
        def src_of(n):
            return xrow.at[place_of(m), rows(n)]

        def step(i, c):
            dx = near_first(3 - i)
            grad_x(wd, m, (x + dx) % 4)
            if at_once:
                spread_at(dx, src_of, ret.at[k, rows(q)], r2_s.at[k], r2_r.at[k, dx])
            return c

        lax.fori_loop(0, 4, step, 0)
        if not at_once:
            spread(src_of, ret.at[k, rows(q)], r2_s.at[k], lambda dx: r2_r.at[k, dx])

    back_own(3, 2, False)
    back_own(0, 1, False)

    def pair_back():
        def step(dx):
            part = chunk((x + dx) % 4)
            for m in (1, 2):
                wait(back.at[m - 1, part], r1_r.at[m - 1, dx])
            pair = back[0, part, :].astype(F32) + back[1, part, :].astype(F32)
            buf[part, :] = pair.astype(BF16)

        each(step)
        spread(
            lambda n: buf.at[rows(n)], ret.at[0, rows(q)], r2_s.at[0],
            lambda dx: r2_r.at[0, dx],
        )

    wait(xrow.at[0], r2_s.at[2])
    for dx in range(4):
        arrived(ret.at[2], (x + 4 - dx) % 4, r2_r.at[2, dx], dx)

    def far_total(n, c):
        here = pl.ds(pl.multiple_of(ROWS + n * PART, PART), PART)
        buf[here, :] = total_own(n, 2).astype(BF16)
        send(buf.at[here], out.at[tokens_of(n)], p3_s.at[n], p3_r.at[n], peer(3))
        return c

    lax.fori_loop(0, 4, far_total, 0)
    pair_back()

    for m in (1, 2, 3):
        wait(pgl.at[m - 1], g1_r.at[m - 1])
    gs[zl] = pgs[0] + pgl[2]
    gs[ozl] = pgl[0] + pgl[1]
    pltpu.make_async_copy(gs, gb.at[q], g2_r).start()

    def send_gate(i, c):
        send(gs, gb.at[q], g2_s, g2_r, dev(zl, (yc + i % 8) % 8, (x + i // 8) % 4, zh))
        return c

    lax.fori_loop(1, 32, send_gate, 0)

    wait(xrow.at[0], r2_s.at[1])
    for dx in range(4):
        arrived(ret.at[1], (x + 4 - dx) % 4, r2_r.at[1, dx], dx)

    def own_total(n, c):
        pre[n, 0:PART, 0:SH] = total_own(n, 1)
        return c

    lax.fori_loop(0, 4, own_total, 0)

    wait(gb, g2_r)
    keep = lax.broadcasted_iota(jnp.int32, (32, 8, 128), 1) == yc
    terms = jnp.concatenate([jnp.sum(jnp.where(keep, gb[:, s], 0.0), axis=1) for s in (0, 1)])
    terms = terms.T
    coarse = terms.astype(BF16)
    fine = (terms - coarse.astype(F32)).astype(BF16)
    lane = lax.broadcasted_iota(jnp.int32, (128, 128), 0).astype(F32)
    for k in (0, 1):
        at = jnp.where(expert == pack[4 + k : 5 + k, :], 1.0, 0.0).astype(BF16)
        found = dot(coarse, at) + dot(fine, at)
        gate_out[k : k + 1, :] = jnp.sum(
            jnp.where(lane == pack[6 + k : 7 + k, :], found, 0.0), axis=0, keepdims=True
        )

    wait(xrow.at[0], r2_s.at[0])

    for dx in range(4):
        arrived(ret.at[0], (x + 4 - dx) % 4, r2_r.at[0, dx], dx)

    def finish(n, c):
        here = tokens_of(n)
        total = pre[n, 0:PART, 0:SH] + total_near(n)
        wait(out.at[here], p3_r.at[n])
        out[here, :] = (total + out[here, :].astype(F32)).astype(BF16)
        wait(out.at[here], p3_s.at[n])
        return c

    lax.fori_loop(0, 4, finish, 0)

    wait(posb.at[pl.ds(0, 15)], pos_s)
    for m in (0, 1, 2):
        wait(pgl.at[m], g1_s.at[m])
    for m in (0, 1):
        wait(dyz.at[m], z_s.at[m])
        wait(back.at[m], r1_s.at[m])
    wait(gb.at[pl.ds(0, 31)], g2_s)


def expert_layer(names, gates, tokens, grad_out, gate_w, up_w, down_w):
    vmem = pl.BlockSpec(memory_space=pltpu.VMEM)
    hbm = pl.BlockSpec(memory_space=pl.ANY)
    dma = pltpu.SemaphoreType.DMA
    return pl.pallas_call(
        kernel,
        name="expert_layer",
        out_shape=(
            jax.ShapeDtypeStruct((TOK, SH), BF16),
            jax.ShapeDtypeStruct((2, 128), F32),
        ),
        in_specs=[vmem, vmem, vmem, vmem, hbm, hbm, hbm],
        out_specs=(vmem, vmem),
        scratch_shapes=[
            pltpu.VMEM((WIDTH, HID), BF16),
            pltpu.VMEM((WIDTH, HID), BF16),
            pltpu.VMEM((HID, WIDTH), BF16),
            pltpu.VMEM((4, ROWS, SH), BF16),
            pltpu.VMEM((4, ROWS, SH), BF16),
            pltpu.VMEM((ROWS, SH), BF16),
            pltpu.VMEM((3 * ROWS, SH), BF16),
            pltpu.VMEM((3, TOK, SH), BF16),
            pltpu.VMEM((2, ROWS, SH), BF16),
            pltpu.VMEM((3, ROWS, SH), BF16),
            pltpu.VMEM((6, CHUNK, HID), F32),
            pltpu.VMEM((CHUNK, 2 * HID), BF16),
            pltpu.VMEM((8, 128), F32),
            pltpu.VMEM((16, 8, 128), F32),
            pltpu.VMEM((TOK, 8), F32),
            pltpu.VMEM((2, 8, 128), F32),
            pltpu.VMEM((3, 8, 128), F32),
            pltpu.VMEM((2, 8, 128), F32),
            pltpu.VMEM((32, 2, 8, 128), F32),
            dma((3,)),
            dma, dma,
            dma((3,)), dma((3, 2)),
            dma((4,)), dma((4,)),
            dma((3,)), dma((3, 4)),
            dma((6,)), dma((4, 4)),
            dma((2,)), dma((2, 4)),
            dma((3,)), dma((3, 4)),
            dma((4,)), dma((4,)),
            dma((3,)), dma((3,)),
            dma, dma,
        ],
        compiler_params=pltpu.CompilerParams(
            collective_id=0, has_side_effects=True, vmem_limit_bytes=64 << 20
        ),
        cost_estimate=pl.CostEstimate(
            flops=36_000_000_000, bytes_accessed=25_000_000, transcendentals=600_000
        ),
    )(names, gates, tokens, grad_out, gate_w, up_w, down_w)


def body(tokens, grad_out, expert_ids, gates, w_gate, w_up, w_down):
    grad_tokens, grad_gates = expert_layer(
        expert_ids.T, gates.T, tokens, grad_out, w_gate[0], w_up[0], w_down[0]
    )
    return (grad_tokens, grad_gates.T)


def solution(mesh):
    placed = (
        P("ctx", "tp"),
        P("ctx", "tp"),
        P(("ctx", "tp"), None),
        P(("ctx", "tp"), None),
        P(("ctx", "tp"), None, None),
        P(("ctx", "tp"), None, None),
        P(("ctx", "tp"), None, None),
    )
    return jax.shard_map(
        body,
        mesh=mesh,
        in_specs=placed,
        out_specs=(P("ctx", "tp"), P(("ctx", "tp"), None)),
        check_vma=False,
    )
```

```python
import functools

import jax
import jax.numpy as jnp
from jax import lax
from jax.experimental import pallas as pl
from jax.experimental.pallas import tpu as pltpu
from jax.sharding import PartitionSpec as P

MESH = pl.DeviceIdType.MESH
STEPS = (
    (2, 2), (1, 0), (0, 1), (2, 1), (3, 0), (0, 3), (1, 2), (2, 3),
    (3, 2), (1, 1), (3, 3), (2, 0), (0, 2), (1, 3), (3, 1), (0, 0),
)
F32 = jnp.float32
BF16 = jnp.bfloat16

CAP = 6
BLK = 48
CHUNK = 384
ROWS = 1536
TOK = 1024
SH = 512
HID = 768
WIDTH = 4096
PART = 256


def dot(left, right):
    return jnp.dot(left, right, preferred_element_type=F32)


def dot_last(left, right):
    return lax.dot_general(left, right, (((1,), (1,)), ((), ())), preferred_element_type=F32)


def kernel(
    names, gates, tok, dy, wg_hbm, wu_hbm, wd_hbm,
    out, gate_out,
    wg, wu, wd, xrow, yrow, stage, buf, dyz, back, ret,
    pre, dab, pack, posb, post, pgs, pgl, gs, gb,
    w_sem, pos_s, pos_r, z_s, z_r, a1x_r, a1p_r, a2_s, a2_r,
    b_s, b2_r, r1_s, r1_r, r2_s, r2_r, p3_s, p3_r, g1_s, g1_r, g2_s, g2_r,
):
    ctx, tp = lax.axis_index("ctx"), lax.axis_index("tp")
    zl, yc, x, zh = ctx // 8, ctx % 8, tp // 2, tp % 2
    ozl = 1 - zl
    plane = zl * 2 + zh
    q = x * 8 + yc

    def dev(zl_, yc_, x_, zh_):
        return (zl_ * 8 + yc_, x_ * 2 + zh_)

    def plane_of(m):
        return (zl + ((m + 1) // 2) % 2) % 2, (zh + m // 2) % 2

    def place_of(m):
        zl_, zh_ = plane_of(m)
        return zl_ * 2 + zh_

    def peer(m):
        zl_, zh_ = plane_of(m)
        return dev(zl_, yc, x, zh_)

    def near_first(i):
        return i + (i // 2) * (5 - 2 * i)

    def rows(n):
        return pl.ds(pl.multiple_of(n * BLK, BLK), BLK)

    def chunk(n):
        return pl.ds(pl.multiple_of(n * CHUNK, CHUNK), CHUNK)

    def shard(n):
        return pl.ds(pl.multiple_of(n * SH, SH), SH)

    def send(src, dst, s_sem, r_sem, to):
        pltpu.make_async_remote_copy(
            src_ref=src, dst_ref=dst, send_sem=s_sem, recv_sem=r_sem,
            device_id=to, device_id_type=MESH,
        ).start()

    def wait(ref, sem):
        pltpu.make_async_copy(ref, ref, sem).wait()

    bar = pltpu.get_barrier_semaphore()

    def greet_plane(i, c):
        to = dev(zl, (yc + i % 8) % 8, (x + i // 8) % 4, zh)
        pl.semaphore_signal(bar, inc=1, device_id=to, device_id_type=MESH)
        return c

    def greet_other(i, c):
        zl_, zh_ = plane_of(1 + i // 4)
        to = dev(zl_, yc, (x + i % 4) % 4, zh_)
        pl.semaphore_signal(bar, inc=1, device_id=to, device_id_type=MESH)
        return c

    lax.fori_loop(0, 12, greet_other, 0)
    lax.fori_loop(1, 32, greet_plane, 0)
    loads = [
        pltpu.make_async_copy(wg_hbm, wg, w_sem.at[0]),
        pltpu.make_async_copy(wu_hbm, wu, w_sem.at[1]),
        pltpu.make_async_copy(wd_hbm, wd, w_sem.at[2]),
    ]
    for load in loads:
        load.start()

    ids = [names[k : k + 1, :].astype(F32) for k in (0, 1)]
    expert = lax.broadcasted_iota(jnp.int32, (64, 128), 0).astype(F32)
    named = [jnp.where(expert == e, 1.0, 0.0) for e in ids]
    before = lax.broadcasted_iota(jnp.int32, (128, 128), 0) < lax.broadcasted_iota(
        jnp.int32, (128, 128), 1
    )
    earlier = dot((named[0] + named[1]).astype(BF16), jnp.where(before, 1.0, 0.0).astype(BF16))
    first = (tp * CAP).astype(F32)
    for k in (0, 1):
        slot = jnp.sum(named[k] * earlier, axis=0, keepdims=True) + first
        half = jnp.floor(ids[k] * (1 / 32))
        rest = ids[k] - half * 32.0
        line = jnp.floor(rest * 0.25)
        column = rest - line * 4.0
        pack[k : k + 1, :] = (half * 4.0 + column) * CHUNK + line * BLK + slot
        pack[2 + k : 3 + k, :] = gates[k : k + 1, :]
        pack[4 + k : 5 + k, :] = half * 32.0 + column * 8.0 + line
        pack[6 + k : 7 + k, :] = slot

    pl.semaphore_wait(bar, 43)

    top, low = pl.ds(0, TOK // 2), pl.ds(TOK // 2, TOK // 2)
    send(dy.at[top], dyz.at[0, top], z_s.at[0], z_r.at[0, 0], peer(1))
    send(dy.at[low], dyz.at[1, low], z_s.at[1], z_r.at[1, 1], peer(2))
    mine = posb.at[zl * 8 + tp]
    pltpu.make_async_copy(pack, mine, pos_r).start()

    def send_pos(i, c):
        to = dev((zl + i // 8) % 2, yc, (x + (i // 2) % 4) % 4, (zh + i % 2) % 2)
        send(pack, mine, pos_s, pos_r, to)
        return c

    lax.fori_loop(1, 16, send_pos, 0)
    wait(posb, pos_r)

    def select(zl_, c):
        place = (lax.broadcasted_iota(jnp.int32, (CHUNK, 128), 0) + c * CHUNK).astype(F32)
        parts = []
        for n in range(8):
            tile = posb[zl_ * 8 + n]
            hit = (place == tile[0:1]) | (place == tile[1:2])
            parts.append(jnp.where(hit, 1.0, 0.0).astype(BF16))
        return jnp.concatenate(parts, axis=1)

    def spread(src_of, dst, s_sem, r_sem_of, steps=STEPS):
        def side(n, c):
            dc = 1 - n
            for dx, dy in steps:
                xd, ycd = (x + dx) % 4, (yc // 2 + dy) % 4 * 2 + (yc + dc) % 2
                src = src_of(xd * 8 + ycd)
                go = functools.partial(
                    send, src, dst, s_sem, r_sem_of(dx), dev(zl, ycd, xd, zh)
                )
                if dx + dy > 0:
                    go()
                    continue

                @pl.when(dc == 0)
                def _():
                    pltpu.make_async_copy(src, dst, s_sem).start()

                pl.when(dc > 0)(go)
            return c

        lax.fori_loop(0, 2, side, 0)

    def spread_at(dx, src_of, dst, s_sem, r_sem):
        xd = (x + dx) % 4

        def one(j, c):
            ycd = (yc + j) % 8
            src = src_of(xd * 8 + ycd)
            own = dx * 8 + j == 0

            @pl.when(own)
            def _():
                pltpu.make_async_copy(src, dst, s_sem).start()

            @pl.when(jnp.logical_not(own))
            def _():
                send(src, dst, s_sem, r_sem, dev(zl, ycd, xd, zh))

            return c

        lax.fori_loop(0, 8, one, 0)

    def arrived(ref, xs, sem, dx):
        @pl.when(dx > 0)
        def _():
            wait(ref.at[chunk(xs)], sem)

        @pl.when(dx == 0)
        def _():
            wait(ref.at[pl.ds(0, CHUNK - BLK)], sem)

    def left(b):
        wait(buf.at[pl.ds(0, ROWS)], b_s.at[b])

    def batch(b, slot, src, zl_src, zl_dst, dst, r_sem_of):
        def gather(first):
            def step(i, c):
                xd = (x + first + 2 * i) % 4
                picked = dot(select(zl_src, zl_dst * 4 + xd), src[...])
                buf[chunk(4 * slot + xd), :] = picked.astype(BF16)
                return c

            lax.fori_loop(0, 2, step, 0)

        def src_of(k):
            return buf.at[rows(32 * slot + k)]

        if b == 0:
            for first in (0, 1):
                gather(first)
                part = [step for step in STEPS if step[0] % 2 == first]
                spread(src_of, dst, b_s.at[b], r_sem_of, part)
        else:
            gather(0)
            gather(1)
            spread(src_of, dst, b_s.at[b], r_sem_of)

    def x_out(b, slot, s):
        dst = stage.at[rows(q)] if s else xrow.at[plane, rows(q)]
        sem = a1p_r if s else a1x_r
        batch(b, slot, tok, zl, (zl + s) % 2, dst, lambda dx: sem.at[dx])

    def y_out(b, slot, m):
        src = dy if m == 0 else dyz.at[m - 1]
        dst = yrow.at[place_of(m), rows(q)]
        batch(b, slot, src, plane_of(m)[0], zl, dst, lambda dx: b2_r.at[m, dx])

    def forward_near(dx):
        xs = (x + 4 - dx) % 4
        part = chunk(xs)
        arrived(stage, xs, a1p_r.at[dx], dx)
        for m in (1, 2):
            send(stage.at[part], xrow.at[plane, part], a2_s.at[m - 1], a2_r.at[m - 1, dx], peer(m))

    def forward_far(dx):
        part = chunk((x + 4 - dx) % 4)
        send(xrow.at[plane, part], xrow.at[plane, part], a2_s.at[2], a2_r.at[2, dx], peer(3))

    def base_of(m):
        return 0 if m in (1, 2) else 3

    def take_x(m, dx):
        xs = (x + 4 - dx) % 4
        src = xrow.at[place_of(m), chunk(xs)]
        if m > 0:
            wait(src, a2_r.at[m - 1, dx])
        part = shard(xs * 2 + plane_of(m)[1])
        pre[base_of(m)] += dot(src[...], wg[part, :])
        pre[base_of(m) + 1] += dot(src[...], wu[part, :])

    def take_y(m, dx):
        xs = (x + 4 - dx) % 4
        arrived(yrow.at[place_of(m)], xs, b2_r.at[m, dx], dx)
        part = shard(xs * 2 + plane_of(m)[1])
        pre[base_of(m) + 2] += dot_last(yrow[place_of(m), chunk(xs), :], wd[:, part])

    def each(f):
        def step(i, c):
            f(near_first(i))
            return c

        lax.fori_loop(0, 4, step, 0)

    x_out(0, 0, 1)
    send(dy.at[low], dyz.at[0, low], z_s.at[0], z_r.at[0, 1], peer(1))
    send(dy.at[top], dyz.at[1, top], z_s.at[1], z_r.at[1, 0], peer(2))
    x_out(1, 1, 0)
    wait(dyz.at[0, top], z_r.at[0, 0])
    send(dyz.at[0, top], dyz.at[2, top], z_s.at[2], z_r.at[2, 0], peer(2))
    wait(dyz.at[1, low], z_r.at[1, 1])
    send(dyz.at[1, low], dyz.at[2, low], z_s.at[2], z_r.at[2, 1], peer(1))
    wait(dyz.at[0, low], z_r.at[0, 1])
    y_out(2, 2, 1)
    left(0)
    for dx in (0, 1, 3, 2):
        forward_near(dx)
    wait(dyz.at[1, top], z_r.at[1, 0])
    y_out(3, 0, 2)
    pre[...] = jnp.zeros_like(pre)
    for load in loads:
        load.wait()
    left(1)
    for dx in (0, 1, 3, 2):
        arrived(xrow.at[plane], (x + 4 - dx) % 4, a1x_r.at[dx], dx)
    each(lambda dx: take_x(0, dx))
    left(2)
    y_out(4, 2, 0)
    each(lambda dx: (take_x(1, dx), take_x(2, dx)))
    for m in (0, 1):
        wait(xrow.at[0], a2_s.at[m])
    for dx in (0, 1, 3, 2):
        forward_far(dx)
    wait(dyz.at[2, top], z_r.at[2, 0])
    wait(dyz.at[2, low], z_r.at[2, 1])
    left(3)
    y_out(5, 0, 3)
    each(lambda dx: take_y(1, dx))
    each(lambda dx: take_y(2, dx))

    def inner(g, dst):
        base = 0 if g else 3

        def step(n, c):
            part = rows(n)
            av, bv, hv = pre[base, part, :], pre[base + 1, part, :], pre[base + 2, part, :]
            sigma = 1.0 / (1.0 + jnp.exp(-av))
            active = av * sigma
            hidden = (active * bv).astype(BF16).astype(F32)
            dst[part, 0:HID] = (hv * bv * sigma * (1.0 + av * (1.0 - sigma))).astype(BF16)
            dst[part, HID : 2 * HID] = (hv * active).astype(BF16)
            gate = jnp.sum(hidden * hv, axis=1, keepdims=True)
            diag = lax.broadcasted_iota(jnp.int32, (BLK, 128), 0) == lax.broadcasted_iota(
                jnp.int32, (BLK, 128), 1
            )
            pgs[g, pl.ds(n, 1), :] = jnp.sum(jnp.where(diag, gate, 0.0), axis=0, keepdims=True)
            return c

        lax.fori_loop(0, 8, step, 0)

    def grad_x(src, m, xs):
        piece = shard(xs * 2 + plane_of(m)[1])
        val = dot_last(src[0:CHUNK, 0:HID], wg[piece, :])
        val += dot_last(src[0:CHUNK, HID : 2 * HID], wu[piece, :])
        here = xrow.at[place_of(m), chunk(xs)]
        here[...] = val.astype(BF16)
        return here

    inner(1, dab)
    for m in (1, 2):
        send(pgs.at[1], pgl.at[m - 1], g1_s.at[m - 1], g1_r.at[m - 1], peer(m))

    def back_near(dx):
        for m in (1, 2):
            grad_x(dab, m, (x + dx) % 4)

    each(back_near)
    left(4)
    each(lambda dx: take_y(0, dx))

    for n in range(8):
        post[pl.ds(n * 128, 128), :] = posb[zl * 8 + n].T

    def tokens_of(n):
        return pl.ds(pl.multiple_of(n * PART, PART), PART)

    def weigh(n, first, size):
        tile = post[tokens_of(n), :]
        place = (lax.broadcasted_iota(jnp.int32, (PART, size), 1) + first).astype(F32)
        hit = jnp.where(place == tile[:, 0:1], tile[:, 2:3], 0.0)
        return (hit + jnp.where(place == tile[:, 1:2], tile[:, 3:4], 0.0)).astype(BF16)

    wait(dyz.at[2], z_s.at[2])

    def weigh_own(n, c):
        for p in range(3):
            dyz[p, tokens_of(n), :] = weigh(n, zl * ROWS + p * SH, SH)
        return c

    lax.fori_loop(0, 4, weigh_own, 0)

    def near_place(n, p):
        if p == 2:
            base = TOK + n % 2 * PART
            late = pl.ds(pl.multiple_of(base, PART), PART)
            return late, pl.ds(pl.multiple_of(2 * ROWS + base, PART), PART)
        base = n * PART
        if p == 1:
            return pl.ds(pl.multiple_of(base, PART), PART), None
        return None, pl.ds(pl.multiple_of(2 * ROWS + base, PART), PART)

    def weigh_near(n, c):
        first = ozl * ROWS
        buf[near_place(n, 0)[1], :] = weigh(n, first, SH)
        stage[near_place(n, 1)[0], :] = weigh(n, first + SH, SH)
        in_stage, in_buf = near_place(n, 2)
        tile = weigh(n, first + 2 * SH, SH)

        @pl.when(n < 2)
        def _():
            stage[in_stage, :] = tile

        @pl.when(n >= 2)
        def _():
            buf[in_buf, :] = tile

        return c

    def total_near(n):
        total = dot(buf[near_place(n, 0)[1], :], ret[0, 0:SH, :])
        total += dot(stage[near_place(n, 1)[0], :], ret[0, SH : 2 * SH, :])
        in_stage, in_buf = near_place(n, 2)
        last = jnp.where(n < 2, stage[in_stage, :], buf[in_buf, :])
        return total + dot(last, ret[0, 2 * SH : 3 * SH, :])


    def total_own(n, k):
        total = dot(dyz[0, tokens_of(n), :], ret[k, 0:SH, :])
        for p in (1, 2):
            total += dot(dyz[p, tokens_of(n), :], ret[k, p * SH : (p + 1) * SH, :])
        return total

    wait(xrow.at[plane], a2_s.at[2])
    for i in (2, 3, 1, 0):
        part = chunk((x + i) % 4)
        for m in (1, 2):
            send(
                xrow.at[place_of(m), part], back.at[m - 1, part],
                r1_s.at[m - 1], r1_r.at[m - 1, i], peer(m),
            )

    lax.fori_loop(0, 4, weigh_near, 0)

    each(lambda dx: take_x(3, dx))
    left(5)
    each(lambda dx: take_y(3, dx))
    inner(0, wd)
    send(pgs.at[0], pgl.at[2], g1_s.at[2], g1_r.at[2], peer(3))

    def back_own(m, k, at_once):
        def src_of(n):
            return xrow.at[place_of(m), rows(n)]

        def step(i, c):
            dx = near_first(3 - i)
            grad_x(wd, m, (x + dx) % 4)
            if at_once:
                spread_at(dx, src_of, ret.at[k, rows(q)], r2_s.at[k], r2_r.at[k, dx])
            return c

        lax.fori_loop(0, 4, step, 0)
        if not at_once:
            spread(src_of, ret.at[k, rows(q)], r2_s.at[k], lambda dx: r2_r.at[k, dx])

    back_own(3, 2, False)
    back_own(0, 1, False)

    def pair_back():
        def step(dx):
            part = chunk((x + dx) % 4)
            for m in (1, 2):
                wait(back.at[m - 1, part], r1_r.at[m - 1, dx])
            pair = back[0, part, :].astype(F32) + back[1, part, :].astype(F32)
            buf[part, :] = pair.astype(BF16)

        each(step)
        spread(
            lambda n: buf.at[rows(n)], ret.at[0, rows(q)], r2_s.at[0],
            lambda dx: r2_r.at[0, dx],
        )

    wait(xrow.at[0], r2_s.at[2])
    for dx in range(4):
        arrived(ret.at[2], (x + 4 - dx) % 4, r2_r.at[2, dx], dx)

    def far_total(n, c):
        here = pl.ds(pl.multiple_of(ROWS + n * PART, PART), PART)
        buf[here, :] = total_own(n, 2).astype(BF16)
        send(buf.at[here], out.at[tokens_of(n)], p3_s.at[n], p3_r.at[n], peer(3))
        return c

    lax.fori_loop(0, 4, far_total, 0)
    pair_back()

    for m in (1, 2, 3):
        wait(pgl.at[m - 1], g1_r.at[m - 1])
    gs[zl] = pgs[0] + pgl[2]
    gs[ozl] = pgl[0] + pgl[1]
    pltpu.make_async_copy(gs, gb.at[q], g2_r).start()

    def send_gate(i, c):
        send(gs, gb.at[q], g2_s, g2_r, dev(zl, (yc + i % 8) % 8, (x + i // 8) % 4, zh))
        return c

    lax.fori_loop(1, 32, send_gate, 0)

    wait(xrow.at[0], r2_s.at[1])
    for dx in range(4):
        arrived(ret.at[1], (x + 4 - dx) % 4, r2_r.at[1, dx], dx)

    def own_total(n, c):
        pre[n, 0:PART, 0:SH] = total_own(n, 1)
        return c

    lax.fori_loop(0, 4, own_total, 0)

    wait(gb, g2_r)
    keep = lax.broadcasted_iota(jnp.int32, (32, 8, 128), 1) == yc
    terms = jnp.concatenate([jnp.sum(jnp.where(keep, gb[:, s], 0.0), axis=1) for s in (0, 1)])
    terms = terms.T
    coarse = terms.astype(BF16)
    fine = (terms - coarse.astype(F32)).astype(BF16)
    lane = lax.broadcasted_iota(jnp.int32, (128, 128), 0).astype(F32)
    for k in (0, 1):
        at = jnp.where(expert == pack[4 + k : 5 + k, :], 1.0, 0.0).astype(BF16)
        found = dot(coarse, at) + dot(fine, at)
        gate_out[k : k + 1, :] = jnp.sum(
            jnp.where(lane == pack[6 + k : 7 + k, :], found, 0.0), axis=0, keepdims=True
        )

    wait(xrow.at[0], r2_s.at[0])

    for dx in range(4):
        arrived(ret.at[0], (x + 4 - dx) % 4, r2_r.at[0, dx], dx)

    def finish(n, c):
        here = tokens_of(n)
        total = pre[n, 0:PART, 0:SH] + total_near(n)
        wait(out.at[here], p3_r.at[n])
        out[here, :] = (total + out[here, :].astype(F32)).astype(BF16)
        wait(out.at[here], p3_s.at[n])
        return c

    lax.fori_loop(0, 4, finish, 0)

    wait(posb.at[pl.ds(0, 15)], pos_s)
    for m in (0, 1, 2):
        wait(pgl.at[m], g1_s.at[m])
    for m in (0, 1):
        wait(dyz.at[m], z_s.at[m])
        wait(back.at[m], r1_s.at[m])
    wait(gb.at[pl.ds(0, 31)], g2_s)


def expert_layer(names, gates, tokens, grad_out, gate_w, up_w, down_w):
    vmem = pl.BlockSpec(memory_space=pltpu.VMEM)
    hbm = pl.BlockSpec(memory_space=pl.ANY)
    dma = pltpu.SemaphoreType.DMA
    return pl.pallas_call(
        kernel,
        name="expert_layer",
        out_shape=(
            jax.ShapeDtypeStruct((TOK, SH), BF16),
            jax.ShapeDtypeStruct((2, 128), F32),
        ),
        in_specs=[vmem, vmem, vmem, vmem, hbm, hbm, hbm],
        out_specs=(vmem, vmem),
        scratch_shapes=[
            pltpu.VMEM((WIDTH, HID), BF16),
            pltpu.VMEM((WIDTH, HID), BF16),
            pltpu.VMEM((HID, WIDTH), BF16),
            pltpu.VMEM((4, ROWS, SH), BF16),
            pltpu.VMEM((4, ROWS, SH), BF16),
            pltpu.VMEM((ROWS, SH), BF16),
            pltpu.VMEM((3 * ROWS, SH), BF16),
            pltpu.VMEM((3, TOK, SH), BF16),
            pltpu.VMEM((2, ROWS, SH), BF16),
            pltpu.VMEM((3, ROWS, SH), BF16),
            pltpu.VMEM((6, CHUNK, HID), F32),
            pltpu.VMEM((CHUNK, 2 * HID), BF16),
            pltpu.VMEM((8, 128), F32),
            pltpu.VMEM((16, 8, 128), F32),
            pltpu.VMEM((TOK, 8), F32),
            pltpu.VMEM((2, 8, 128), F32),
            pltpu.VMEM((3, 8, 128), F32),
            pltpu.VMEM((2, 8, 128), F32),
            pltpu.VMEM((32, 2, 8, 128), F32),
            dma((3,)),
            dma, dma,
            dma((3,)), dma((3, 2)),
            dma((4,)), dma((4,)),
            dma((3,)), dma((3, 4)),
            dma((6,)), dma((4, 4)),
            dma((2,)), dma((2, 4)),
            dma((3,)), dma((3, 4)),
            dma((4,)), dma((4,)),
            dma((3,)), dma((3,)),
            dma, dma,
        ],
        compiler_params=pltpu.CompilerParams(
            collective_id=0, has_side_effects=True, vmem_limit_bytes=64 << 20
        ),
        cost_estimate=pl.CostEstimate(
            flops=36_000_000_000, bytes_accessed=25_000_000, transcendentals=600_000
        ),
    )(names, gates, tokens, grad_out, gate_w, up_w, down_w)


def body(tokens, grad_out, expert_ids, gates, w_gate, w_up, w_down):
    grad_tokens, grad_gates = expert_layer(
        expert_ids.T, gates.T, tokens, grad_out, w_gate[0], w_up[0], w_down[0]
    )
    return (grad_tokens, grad_gates.T)


def solution(mesh):
    placed = (
        P("ctx", "tp"),
        P("ctx", "tp"),
        P(("ctx", "tp"), None),
        P(("ctx", "tp"), None),
        P(("ctx", "tp"), None, None),
        P(("ctx", "tp"), None, None),
        P(("ctx", "tp"), None, None),
    )
    return jax.shard_map(
        body,
        mesh=mesh,
        in_specs=placed,
        out_specs=(P("ctx", "tp"), P(("ctx", "tp"), None)),
        check_vma=False,
    )
```
